256 devices in a mesh: section: 16 (over z, core), tp: 16 (over x, y).
Axes of the slice: x: 4, y: 4, z: 8, core: 2. Of those that a mesh axis runs over, the one named last changes fastest.
Arguments:
- patches: bfloat16 [1024, 1664], P(('section', 'tp')), may hold values from -6 to 6
- vit_gain: float32 [1664], replicated, may hold values from 0.1 to 1.9
- vit_up: bfloat16 [1664, 4096], P(None, 'tp'), may hold values from -0.15625 to 0.15625
- vit_down: bfloat16 [4096, 1664], P('tp'), may hold values from -0.1875 to 0.1875
- project: bfloat16 [1664, 8192], P(None, 'tp'), may hold values from -0.4375 to 0.4375
- text: bfloat16 [256, 8192], P(None, 'tp'), may hold values from -6 to 6
- image_counts: int32 [16], replicated, may hold values from 1 to 16, as said below
- image_dest: int32 [16, 16], replicated, may hold values from 0 to 255, as said below
- layer_gain: bfloat16 [16, 8192], P('section', 'tp'), may hold values from 0.25 to 1.75
- layer_weight: bfloat16 [16, 8192, 8192], P('section', None, 'tp'), may hold values from -0.0625 to 0.0625
Outputs:
- section_outputs: bfloat16 [16, 8, 32, 8192], P('section', None, None, 'tp')
The draws below stay inside these ranges and needn't reach their ends.
Inputs may be any that keep to these rules, and one draw needn't show every extreme that they name: Section s uses the first image_counts[s] of its 16 slots; at least one section uses all 16. `image_dest`: all entries are distinct.
All inputs are finite; a program needn't handle non-finite values.
Results may differ from the reference program's by a relative error of at most 0.024.
Values may be sent and summed in bfloat16 or wider, within the bound.
A program may use at most 64 MiB of HBM per device.

```python
import jax
import jax.numpy as jnp
from jax import lax

D = 8192
DV = 1664
FV = 4096
POOL = 4
MB = 8
SEQ = 32
VIS = 1024
CAP = 16
ROWS = 256
N_SECTION = 16


def draw_image_counts(key, part):
    key = jax.random.fold_in(key, 11)
    first, second, third = jax.random.split(key, 3)
    left = jax.random.randint(first, (N_SECTION,), 0, CAP)
    right = jax.random.randint(second, (N_SECTION,), 0, CAP)
    counts = 1 + left * right // CAP
    full_section = jax.random.randint(third, (), 0, N_SECTION)
    counts = counts.at[full_section].set(CAP)
    return counts.astype(jnp.int32)


def draw_image_dest(key, part):
    key = jax.random.fold_in(key, 23)
    order = jax.random.permutation(key, ROWS).astype(jnp.int32)
    top_place = jnp.argmax(order == ROWS - 1)
    swapped = order.at[top_place].set(order[0]).at[0].set(ROWS - 1)
    return swapped[:N_SECTION * CAP].reshape(N_SECTION, CAP).astype(jnp.int32)


def block_levels(stream_key, dims, shards, low, largest):
    loudness, own = 1.0, jax.random.fold_in(stream_key, 6)
    for dim, shards_of in shards:
        draws = jnp.exp(jax.random.uniform(jax.random.fold_in(own, dim), (shards_of,), jnp.float32, low / len(shards), largest / len(shards)))
        loudness = loudness * jnp.repeat(draws, dims[dim] // shards_of).reshape([-1 if axis == dim else 1 for axis in range(len(dims))])
    return loudness


def gaussian(stream_key, shape, width, most, cuts=(), kind=jnp.bfloat16):
    values = width * jax.random.normal(stream_key, shape, jnp.float32)
    if cuts:
        values = values * block_levels(stream_key, shape, cuts, -0.22, 0.18)
    return jnp.clip(values, -most, most).astype(kind)


def setup_inputs(seed: int = 0) -> dict:
    arg_keys = jax.random.split(jax.random.key(seed), 11)
    patches = gaussian(arg_keys[0], (VIS, DV), 1.0, 6.0, ((0, 256),))
    vit_gain = jnp.clip(1.0 + 0.18 * jax.random.normal(arg_keys[1], (DV,), jnp.float32), 0.1, 1.9)
    vit_up = gaussian(arg_keys[2], (DV, FV), DV ** -0.5, 0.15625, ((1, 16),))
    vit_down = gaussian(arg_keys[3], (FV, DV), (FV // 4) ** -0.5, 0.1875, ((0, 16),))
    project = gaussian(arg_keys[4], (DV, D), (DV // 9) ** -0.5, 0.4375, ((1, 16),))
    text = gaussian(arg_keys[5], (ROWS, D), 1.0, 6.0, ((1, 16),))
    image_counts = draw_image_counts(jax.random.fold_in(arg_keys[10], 71), 0)
    image_dest = draw_image_dest(jax.random.fold_in(arg_keys[10], 71), 0)
    layer_gain = jnp.clip(1.0 + 0.15 * jax.random.normal(arg_keys[8], (N_SECTION, D), jnp.float32), 0.25, 1.75).astype(jnp.bfloat16)
    layer_weight = gaussian(arg_keys[9], (N_SECTION, D, D), D ** -0.5, 0.0625, ((0, 16), (2, 16)))
    return dict(patches=patches, vit_gain=vit_gain, vit_up=vit_up, vit_down=vit_down, project=project, text=text, image_counts=image_counts, image_dest=image_dest, layer_gain=layer_gain, layer_weight=layer_weight)


def reference(patches, vit_gain, vit_up, vit_down, project, text, image_counts, image_dest, layer_gain, layer_weight):
    values = patches.astype(jnp.float32)
    centre = lax.optimization_barrier(jnp.mean(values, axis=1, keepdims=True))
    centred = values - centre
    spread = lax.optimization_barrier(jnp.mean(centred * centred, axis=1, keepdims=True))
    normed = (centred * lax.rsqrt(spread + 1e-05) * vit_gain).astype(jnp.bfloat16)
    hidden = jax.nn.gelu(jnp.dot(normed, vit_up, preferred_element_type=jnp.float32), approximate=True).astype(jnp.bfloat16)
    encoded = values + jnp.dot(hidden, vit_down, preferred_element_type=jnp.float32)
    pooled = lax.optimization_barrier(jnp.mean(encoded.reshape(-1, POOL, DV), axis=1)).astype(jnp.bfloat16)
    embeds = jnp.dot(pooled, project, preferred_element_type=jnp.float32).astype(jnp.bfloat16)
    slots = jnp.arange(CAP, dtype=jnp.int32)
    live = (slots[None, :] < image_counts[:, None]).reshape(-1)
    positions = jnp.arange(ROWS, dtype=jnp.int32)
    onehot = ((image_dest.reshape(-1)[:, None] == positions[None, :]) & live[:, None]).astype(jnp.float32)
    placed = lax.dot_general(onehot, embeds.astype(jnp.float32), (((0,), (0,)), ((), ())), precision=lax.Precision.HIGHEST)
    start_rows = (text.astype(jnp.float32) + placed).astype(jnp.bfloat16)

    def layer(active, params):
        gain, weight = params
        active_f = active.astype(jnp.float32)
        scale = lax.rsqrt(lax.optimization_barrier(jnp.mean(active_f * active_f, axis=1, keepdims=True)) + 1e-05)
        scaled = (active_f * gain.astype(jnp.float32)).astype(jnp.bfloat16)
        product = jnp.dot(scaled, weight, preferred_element_type=jnp.float32)
        result = (active_f + product * scale).astype(jnp.bfloat16)
        return (result, result)
    _, outputs = lax.scan(layer, start_rows, (layer_gain, layer_weight))
    return outputs.reshape(N_SECTION, MB, SEQ, D)
```

```python
import functools

import jax
import jax.numpy as jnp
from jax import lax
from jax.experimental import pallas as pl
from jax.experimental.pallas import tpu as pltpu
from jax.sharding import PartitionSpec as P

MESH = pl.DeviceIdType.MESH
F32 = jnp.float32
BF16 = jnp.bfloat16

D = 8192
DV = 1664
POOL = 4
EPSILON = 1e-05
SIDE = 4
TP = SIDE * SIDE
SECTIONS = 16
ROWS = 256
CAP = 16
WIDTH = D // TP
LANES = 128
COLS = DV // LANES
R = 16
STEPS = ROWS // R
AHEAD = 2


def hops(offset):
    return sum(min(o, SIDE - o) for o in offset)


OFFSETS = sorted(((a, b) for a in range(SIDE) for b in range(SIDE)), key=hops)


def slot_at_target(offset):
    return OFFSETS.index(tuple((SIDE - o) % SIDE for o in offset))


def kernel(
    patches,
    vit_gain,
    counts,
    dest,
    layer_gain,
    vit_up,
    vit_down,
    project,
    text,
    weight,
    out,
    up_v,
    down_v,
    project_v,
    text_v,
    weight_v,
    normed,
    partial,
    parts,
    pooled,
    embed_own,
    embeds,
    onehot,
    start,
    gain_own,
    gains,
    features,
    load_sem,
    weight_sem,
    send_sem,
    normed_sem,
    parts_sem,
    pooled_sem,
    gain_sem,
    embed_sem,
    start_send,
    layer_send,
    feature_sem,
):
    section = lax.axis_index("section")
    me = lax.axis_index("tp")
    x, y = me // SIDE, me % SIDE

    def at(offset):
        return (x + offset[0]) % SIDE * SIDE + (y + offset[1]) % SIDE

    loads = [
        pltpu.make_async_copy(source, target, load_sem.at[i])
        for i, (source, target) in enumerate(
            ((vit_up, up_v), (vit_down, down_v), (project, project_v), (text, text_v))
        )
    ]
    for load in loads:
        load.start()
    for i, offset in enumerate(OFFSETS):
        pltpu.make_async_copy(
            weight.at[pl.ds(pl.multiple_of(at(offset) * WIDTH, WIDTH), WIDTH)],
            weight_v.at[i],
            weight_sem,
        ).start()

    barrier = pltpu.get_barrier_semaphore()

    def greet(to_section, to):
        pl.semaphore_signal(barrier, inc=1, device_id=(to_section, to), device_id_type=MESH)

    for offset in OFFSETS[1:]:
        greet(section, at(offset))

    @pl.when(section > 0)
    def _():
        for offset in OFFSETS:
            greet(section - 1, at(offset))

    @pl.when(section == 0)
    def _():
        for other in range(1, SECTIONS):
            greet(other, me)

    values = patches[...].astype(F32)
    centred = values - jnp.mean(values, axis=1, keepdims=True)
    spread = jnp.mean(centred * centred, axis=1, keepdims=True)
    normed[me] = (centred * lax.rsqrt(spread + EPSILON) * vit_gain[...]).astype(BF16)
    residual = jnp.mean(values, axis=0, keepdims=True)
    gain_own[...] = layer_gain[...].astype(F32)
    gains[0] = layer_gain[...].astype(F32)

    peers = TP - 1 + jnp.where(section < SECTIONS - 1, TP, 0) + jnp.where(section > 0, 1, 0)
    pl.semaphore_wait(barrier, peers)

    def send(source, target, recv_sem, to, sem, to_section=section):
        copy = pltpu.make_async_remote_copy(
            src_ref=source,
            dst_ref=target,
            send_sem=sem,
            recv_sem=recv_sem,
            device_id=(to_section, to),
            device_id_type=MESH,
        )
        copy.start()
        return copy

    def arrived(target, sem):
        pltpu.make_async_copy(target, target, sem).wait()

    sent = []
    for i, offset in reversed(list(enumerate(OFFSETS))[1:]):
        sent.append(
            send(normed.at[me], normed.at[me], normed_sem.at[me], at(offset), send_sem.at[0, i])
        )
    for i, offset in reversed(list(enumerate(OFFSETS))[1:]):
        slot = slot_at_target(offset)
        sent.append(
            send(gain_own, gains.at[slot], gain_sem.at[slot], at(offset), send_sem.at[1, i])
        )

    @pl.when(section == 0)
    def _():
        square = (CAP, CAP)
        spots = lax.broadcasted_iota(jnp.int32, square, 1)
        groups = lax.broadcasted_iota(jnp.int32, square, 0)
        limits = jnp.sum(
            jnp.where(spots == groups, counts[...].astype(F32), 0.0), axis=1, keepdims=True
        )
        wanted = jnp.where(spots.astype(F32) < limits, dest[...].astype(F32), -1.0)
        flat = (CAP, SECTIONS * CAP)
        column = lax.broadcasted_iota(jnp.int32, flat, 1)
        line = lax.broadcasted_iota(jnp.int32, flat, 0)
        spread_out = jnp.dot(
            wanted.astype(BF16), (column % CAP == line).astype(BF16), preferred_element_type=F32
        )
        targets = jnp.sum(
            jnp.where(column // CAP == line, spread_out, 0.0), axis=0, keepdims=True
        )
        rows = lax.broadcasted_iota(jnp.int32, (ROWS, SECTIONS * CAP), 0).astype(F32)
        onehot[...] = (rows == targets).astype(BF16)

    loads[0].wait()
    loads[1].wait()
    for offset in OFFSETS[1:]:
        source = at(offset)
        arrived(normed.at[source], normed_sem.at[source])
    whole = normed[...].reshape(TP * POOL, DV)
    hidden = jax.nn.gelu(
        jnp.dot(whole, up_v[...], preferred_element_type=F32), approximate=True
    ).astype(BF16)
    merge = lax.broadcasted_iota(jnp.int32, (TP, TP * POOL), 1) // POOL == lax.broadcasted_iota(
        jnp.int32, (TP, TP * POOL), 0
    )
    merged = jnp.dot(
        jnp.where(merge, 1.0 / POOL, 0.0).astype(BF16), hidden, preferred_element_type=F32
    )
    terms = jnp.dot(merged.astype(BF16), down_v[...], preferred_element_type=F32)
    mine = lax.broadcasted_iota(jnp.int32, (TP, DV), 0) == me
    terms = (terms + jnp.where(mine, residual, 0.0)).astype(BF16)
    for j in range(COLS):
        partial[j] = terms[:, j * LANES : (j + 1) * LANES]

    for i, offset in reversed(list(enumerate(OFFSETS))[1:]):
        to = at(offset)

        @pl.when(to < COLS)
        def _():
            send(partial.at[to], parts.at[me], parts_sem.at[me], to, send_sem.at[2, i])

    @pl.when(me < COLS)
    def _():
        parts[me] = partial[me]
        for offset in OFFSETS[1:]:
            source = at(offset)
            arrived(parts.at[source], parts_sem.at[source])
        total = jnp.sum(parts[...].astype(F32), axis=0)
        block = pl.ds(pl.multiple_of(me * LANES, LANES), LANES)
        pooled[:, block] = total.astype(BF16)
        for i, offset in reversed(list(enumerate(OFFSETS))[1:]):
            send(
                pooled.at[:, block],
                pooled.at[:, block],
                pooled_sem.at[me],
                at(offset),
                send_sem.at[3, i],
            )

    loads[2].wait()
    for offset in OFFSETS[1:]:
        source = at(offset)

        @pl.when(source < COLS)
        def _():
            block = pl.ds(pl.multiple_of(source * LANES, LANES), LANES)
            arrived(pooled.at[:, block], pooled_sem.at[source])

    embed = jnp.dot(pooled[...], project_v[...], preferred_element_type=F32).astype(BF16)

    @pl.when(section > 0)
    def _():
        embed_own[...] = embed
        send(embed_own, embeds.at[section], embed_sem.at[section], me, send_sem.at[4, 0], 0)

    loads[3].wait()

    def start_rows(m):
        rows = pl.ds(pl.multiple_of(m * R, R), R)
        placed = jnp.dot(
            onehot[rows, :],
            embeds[...].reshape(SECTIONS * CAP, WIDTH),
            preferred_element_type=F32,
        )
        first = (text_v[rows, :].astype(F32) + placed).astype(BF16)
        start[rows, :] = first
        features[m, 0] = first
        for offset in reversed(OFFSETS[1:]):
            slot = slot_at_target(offset)
            send(
                start.at[rows, :],
                features.at[m, slot],
                feature_sem.at[m, slot],
                at(offset),
                start_send.at[m],
            )

    @pl.when(section == 0)
    def _():
        embeds[0] = embed
        for other in range(1, SECTIONS):
            arrived(embeds.at[other], embed_sem.at[other])
        for m in range(AHEAD):
            start_rows(m)

    for i in range(1, TP):
        arrived(gains.at[i], gain_sem.at[i])
    arrived(weight_v, weight_sem)

    def step(m, carry):
        @pl.when((section == 0) & (m + AHEAD < STEPS))
        def _():
            start_rows(m + AHEAD)

        @pl.when(section > 0)
        def _():
            arrived(features.at[m, 0], feature_sem.at[m, 0])

        product = jnp.zeros((R, WIDTH), F32)
        squares = jnp.zeros((R, LANES), F32)
        for i in range(TP):
            if i:
                arrived(features.at[m, i], feature_sem.at[m, i])
            part = features[m, i].astype(F32)
            for c in range(0, WIDTH, LANES):
                squares += part[:, c : c + LANES] * part[:, c : c + LANES]
            scaled = (part * gains[i]).astype(BF16)
            product += jnp.dot(scaled, weight_v[i], preferred_element_type=F32)
        scale = lax.rsqrt(jnp.sum(squares, axis=1, keepdims=True) / D + EPSILON)
        rows = pl.ds(pl.multiple_of(m * R, R), R)
        out[rows, :] = (features[m, 0].astype(F32) + product * scale).astype(BF16)

        @pl.when(section < SECTIONS - 1)
        def _():
            for offset in reversed(OFFSETS):
                slot = slot_at_target(offset)
                send(
                    out.at[rows, :],
                    features.at[m, slot],
                    feature_sem.at[m, slot],
                    at(offset),
                    layer_send.at[m],
                    section + 1,
                )

        return carry

    lax.fori_loop(0, STEPS, step, 0)

    for copy in sent:
        copy.wait_send()
    for i, offset in list(enumerate(OFFSETS))[1:]:
        to = at(offset)

        @pl.when(to < COLS)
        def _():
            arrived(partial.at[0], send_sem.at[2, i])

        @pl.when(me < COLS)
        def _():
            arrived(partial.at[0], send_sem.at[3, i])

    @pl.when(section > 0)
    def _():
        arrived(embed_own, send_sem.at[4, 0])

    def drain(m, carry):
        @pl.when(section == 0)
        def _():
            arrived(features.at[m, pl.ds(0, TP - 1)], start_send.at[m])

        @pl.when(section < SECTIONS - 1)
        def _():
            arrived(features.at[m], layer_send.at[m])

        return carry

    lax.fori_loop(0, STEPS, drain, 0)


def shards(
    patches,
    vit_gain,
    vit_up,
    vit_down,
    project,
    text,
    image_counts,
    image_dest,
    layer_gain,
    layer_weight,
):
    vmem = pl.BlockSpec(memory_space=pltpu.VMEM)
    anywhere = pl.BlockSpec(memory_space=pl.ANY)
    dma = pltpu.SemaphoreType.DMA
    hidden = vit_up.shape[1]
    outputs = pl.pallas_call(
        kernel,
        out_shape=jax.ShapeDtypeStruct((ROWS, WIDTH), BF16),
        in_specs=[vmem] * 5 + [anywhere] * 5,
        out_specs=vmem,
        scratch_shapes=[
            pltpu.VMEM((DV, hidden), BF16),
            pltpu.VMEM((hidden, DV), BF16),
            pltpu.VMEM((DV, WIDTH), BF16),
            pltpu.VMEM((ROWS, WIDTH), BF16),
            pltpu.VMEM((TP, WIDTH, WIDTH), BF16),
            pltpu.VMEM((TP, POOL, DV), BF16),
            pltpu.VMEM((COLS, TP, LANES), BF16),
            pltpu.VMEM((TP, TP, LANES), BF16),
            pltpu.VMEM((TP, DV), BF16),
            pltpu.VMEM((CAP, WIDTH), BF16),
            pltpu.VMEM((SECTIONS, CAP, WIDTH), BF16),
            pltpu.VMEM((ROWS, SECTIONS * CAP), BF16),
            pltpu.VMEM((ROWS, WIDTH), BF16),
            pltpu.VMEM((1, WIDTH), F32),
            pltpu.VMEM((TP, 1, WIDTH), F32),
            pltpu.VMEM((STEPS, TP, R, WIDTH), BF16),
            dma((4,)),
            dma,
            dma((5, TP)),
            dma((TP,)),
            dma((TP,)),
            dma((TP,)),
            dma((TP,)),
            dma((SECTIONS,)),
            dma((STEPS,)),
            dma((STEPS,)),
            dma((STEPS, TP)),
        ],
        compiler_params=pltpu.CompilerParams(
            collective_id=0, has_side_effects=True, vmem_limit_bytes=40 << 20
        ),
        cost_estimate=pl.CostEstimate(
            flops=2 * ROWS * D * WIDTH, bytes_accessed=12 << 20, transcendentals=0
        ),
        name="encoder_and_layers",
    )(
        patches,
        vit_gain[None],
        image_counts[None],
        image_dest,
        layer_gain,
        vit_up,
        vit_down,
        project,
        text,
        layer_weight[0],
    )
    return outputs.reshape(1, 8, ROWS // 8, WIDTH)


def solution(mesh):
    in_specs = (
        P(("section", "tp"), None),
        P(),
        P(None, "tp"),
        P("tp", None),
        P(None, "tp"),
        P(None, "tp"),
        P(),
        P(),
        P("section", "tp"),
        P("section", None, "tp"),
    )
    out_specs = P("section", None, None, "tp")
    return jax.shard_map(shards, mesh=mesh, in_specs=in_specs, out_specs=out_specs, check_vma=False)
```

```python
import functools

import jax
import jax.numpy as jnp
from jax import lax
from jax.experimental import pallas as pl
from jax.experimental.pallas import tpu as pltpu
from jax.sharding import PartitionSpec as P

MESH = pl.DeviceIdType.MESH
F32 = jnp.float32
BF16 = jnp.bfloat16

D = 8192
DV = 1664
POOL = 4
EPSILON = 1e-05
SIDE = 4
TP = SIDE * SIDE
SECTIONS = 16
ROWS = 256
CAP = 16
WIDTH = D // TP
LANES = 128
COLS = DV // LANES
R = 16
STEPS = ROWS // R
AHEAD = 2


def hops(offset):
    return sum(min(o, SIDE - o) for o in offset)


OFFSETS = sorted(((a, b) for a in range(SIDE) for b in range(SIDE)), key=hops)


def slot_at_target(offset):
    return OFFSETS.index(tuple((SIDE - o) % SIDE for o in offset))


def kernel(
    patches_in,
    vit_gain_in,
    counts_in,
    dest_in,
    layer_gain_in,
    vit_up,
    vit_down,
    project,
    text,
    weight,
    out,
    patches,
    vit_gain,
    counts,
    dest,
    layer_gain,
    up_v,
    down_v,
    project_v,
    text_v,
    weight_v,
    normed,
    partial,
    parts,
    pooled,
    embed_own,
    embeds,
    onehot,
    start,
    gain_own,
    gains,
    features,
    load_sem,
    weight_sem,
    send_sem,
    normed_sem,
    parts_sem,
    pooled_sem,
    gain_sem,
    embed_sem,
    start_send,
    layer_send,
    feature_sem,
):
    section = lax.axis_index("section")
    me = lax.axis_index("tp")
    x, y = me // SIDE, me % SIDE

    def at(offset):
        return (x + offset[0]) % SIDE * SIDE + (y + offset[1]) % SIDE

    loads = [
        pltpu.make_async_copy(source, target, load_sem.at[i])
        for i, (source, target) in enumerate(
            (
                (patches_in, patches),
                (vit_gain_in, vit_gain),
                (layer_gain_in, layer_gain),
                (counts_in, counts),
                (dest_in, dest),
                (vit_up, up_v),
                (vit_down, down_v),
                (project, project_v),
                (text, text_v),
            )
        )
    ]
    for load in loads:
        load.start()
    for i, offset in enumerate(OFFSETS):
        pltpu.make_async_copy(
            weight.at[pl.ds(pl.multiple_of(at(offset) * WIDTH, WIDTH), WIDTH)],
            weight_v.at[i],
            weight_sem,
        ).start()

    barrier = pltpu.get_barrier_semaphore()

    def greet(to_section, to):
        pl.semaphore_signal(barrier, inc=1, device_id=(to_section, to), device_id_type=MESH)

    for offset in OFFSETS[1:]:
        greet(section, at(offset))

    @pl.when(section > 0)
    def _():
        for offset in OFFSETS:
            greet(section - 1, at(offset))

    @pl.when(section == 0)
    def _():
        for other in range(1, SECTIONS):
            greet(other, me)

    for load in loads[:3]:
        load.wait()
    values = patches[...].astype(F32)
    centred = values - jnp.mean(values, axis=1, keepdims=True)
    spread = jnp.mean(centred * centred, axis=1, keepdims=True)
    normed[me] = (centred * lax.rsqrt(spread + EPSILON) * vit_gain[...][None]).astype(BF16)
    residual = jnp.mean(values, axis=0, keepdims=True)
    gain_own[...] = layer_gain[...].astype(F32)
    gains[0] = layer_gain[...].astype(F32)

    peers = TP - 1 + jnp.where(section < SECTIONS - 1, TP, 0) + jnp.where(section > 0, 1, 0)
    pl.semaphore_wait(barrier, peers)

    def send(source, target, recv_sem, to, sem, to_section=section):
        copy = pltpu.make_async_remote_copy(
            src_ref=source,
            dst_ref=target,
            send_sem=sem,
            recv_sem=recv_sem,
            device_id=(to_section, to),
            device_id_type=MESH,
        )
        copy.start()
        return copy

    def arrived(target, sem):
        pltpu.make_async_copy(target, target, sem).wait()

    sent = []
    for i, offset in reversed(list(enumerate(OFFSETS))[1:]):
        sent.append(
            send(normed.at[me], normed.at[me], normed_sem.at[me], at(offset), send_sem.at[0, i])
        )
    for i, offset in reversed(list(enumerate(OFFSETS))[1:]):
        slot = slot_at_target(offset)
        sent.append(
            send(gain_own, gains.at[slot], gain_sem.at[slot], at(offset), send_sem.at[1, i])
        )

    loads[3].wait()
    loads[4].wait()

    @pl.when(section == 0)
    def _():
        square = (CAP, CAP)
        spots = lax.broadcasted_iota(jnp.int32, square, 1)
        groups = lax.broadcasted_iota(jnp.int32, square, 0)
        limits = jnp.sum(
            jnp.where(spots == groups, counts[...][None].astype(F32), 0.0), axis=1, keepdims=True
        )
        wanted = jnp.where(spots.astype(F32) < limits, dest[...].astype(F32), -1.0)
        flat = (CAP, SECTIONS * CAP)
        column = lax.broadcasted_iota(jnp.int32, flat, 1)
        line = lax.broadcasted_iota(jnp.int32, flat, 0)
        spread_out = jnp.dot(
            wanted.astype(BF16), (column % CAP == line).astype(BF16), preferred_element_type=F32
        )
        targets = jnp.sum(
            jnp.where(column // CAP == line, spread_out, 0.0), axis=0, keepdims=True
        )
        rows = lax.broadcasted_iota(jnp.int32, (ROWS, SECTIONS * CAP), 0).astype(F32)
        onehot[...] = (rows == targets).astype(BF16)

    loads[5].wait()
    loads[6].wait()
    for offset in OFFSETS[1:]:
        source = at(offset)
        arrived(normed.at[source], normed_sem.at[source])
    whole = normed[...].reshape(TP * POOL, DV)
    hidden = jax.nn.gelu(
        jnp.dot(whole, up_v[...], preferred_element_type=F32), approximate=True
    ).astype(BF16)
    merge = lax.broadcasted_iota(jnp.int32, (TP, TP * POOL), 1) // POOL == lax.broadcasted_iota(
        jnp.int32, (TP, TP * POOL), 0
    )
    merged = jnp.dot(
        jnp.where(merge, 1.0 / POOL, 0.0).astype(BF16), hidden, preferred_element_type=F32
    )
    terms = jnp.dot(merged.astype(BF16), down_v[...], preferred_element_type=F32)
    mine = lax.broadcasted_iota(jnp.int32, (TP, DV), 0) == me
    terms = (terms + jnp.where(mine, residual, 0.0)).astype(BF16)
    for j in range(COLS):
        partial[j] = terms[:, j * LANES : (j + 1) * LANES]

    for i, offset in reversed(list(enumerate(OFFSETS))[1:]):
        to = at(offset)

        @pl.when(to < COLS)
        def _():
            send(partial.at[to], parts.at[me], parts_sem.at[me], to, send_sem.at[2, i])

    @pl.when(me < COLS)
    def _():
        parts[me] = partial[me]
        for offset in OFFSETS[1:]:
            source = at(offset)
            arrived(parts.at[source], parts_sem.at[source])
        total = jnp.sum(parts[...].astype(F32), axis=0)
        block = pl.ds(pl.multiple_of(me * LANES, LANES), LANES)
        pooled[:, block] = total.astype(BF16)
        for i, offset in reversed(list(enumerate(OFFSETS))[1:]):
            send(
                pooled.at[:, block],
                pooled.at[:, block],
                pooled_sem.at[me],
                at(offset),
                send_sem.at[3, i],
            )

    loads[7].wait()
    for offset in OFFSETS[1:]:
        source = at(offset)

        @pl.when(source < COLS)
        def _():
            block = pl.ds(pl.multiple_of(source * LANES, LANES), LANES)
            arrived(pooled.at[:, block], pooled_sem.at[source])

    embed = jnp.dot(pooled[...], project_v[...], preferred_element_type=F32).astype(BF16)

    @pl.when(section > 0)
    def _():
        embed_own[...] = embed
        send(embed_own, embeds.at[section], embed_sem.at[section], me, send_sem.at[4, 0], 0)

    loads[8].wait()

    def start_rows(m):
        rows = pl.ds(pl.multiple_of(m * R, R), R)
        placed = jnp.dot(
            onehot[rows, :],
            embeds[...].reshape(SECTIONS * CAP, WIDTH),
            preferred_element_type=F32,
        )
        first = (text_v[rows, :].astype(F32) + placed).astype(BF16)
        start[rows, :] = first
        features[m, 0] = first
        for offset in reversed(OFFSETS[1:]):
            slot = slot_at_target(offset)
            send(
                start.at[rows, :],
                features.at[m, slot],
                feature_sem.at[m, slot],
                at(offset),
                start_send.at[m],
            )

    @pl.when(section == 0)
    def _():
        embeds[0] = embed
        for other in range(1, SECTIONS):
            arrived(embeds.at[other], embed_sem.at[other])
        for m in range(AHEAD):
            start_rows(m)

    for i in range(1, TP):
        arrived(gains.at[i], gain_sem.at[i])
    arrived(weight_v, weight_sem)

    def step(m, carry):
        @pl.when((section == 0) & (m + AHEAD < STEPS))
        def _():
            start_rows(m + AHEAD)

        @pl.when(section > 0)
        def _():
            arrived(features.at[m, 0], feature_sem.at[m, 0])

        product = jnp.zeros((R, WIDTH), F32)
        squares = jnp.zeros((R, LANES), F32)
        for i in range(TP):
            if i:
                arrived(features.at[m, i], feature_sem.at[m, i])
            part = features[m, i].astype(F32)
            for c in range(0, WIDTH, LANES):
                squares += part[:, c : c + LANES] * part[:, c : c + LANES]
            scaled = (part * gains[i]).astype(BF16)
            product += jnp.dot(scaled, weight_v[i], preferred_element_type=F32)
        scale = lax.rsqrt(jnp.sum(squares, axis=1, keepdims=True) / D + EPSILON)
        rows = pl.ds(pl.multiple_of(m * R, R), R)
        out[rows, :] = (features[m, 0].astype(F32) + product * scale).astype(BF16)

        @pl.when(section < SECTIONS - 1)
        def _():
            for offset in reversed(OFFSETS):
                slot = slot_at_target(offset)
                send(
                    out.at[rows, :],
                    features.at[m, slot],
                    feature_sem.at[m, slot],
                    at(offset),
                    layer_send.at[m],
                    section + 1,
                )

        return carry

    lax.fori_loop(0, STEPS, step, 0)

    for copy in sent:
        copy.wait_send()
    for i, offset in list(enumerate(OFFSETS))[1:]:
        to = at(offset)

        @pl.when(to < COLS)
        def _():
            arrived(partial.at[0], send_sem.at[2, i])

        @pl.when(me < COLS)
        def _():
            arrived(partial.at[0], send_sem.at[3, i])

    @pl.when(section > 0)
    def _():
        arrived(embed_own, send_sem.at[4, 0])

    def drain(m, carry):
        @pl.when(section == 0)
        def _():
            arrived(features.at[m, pl.ds(0, TP - 1)], start_send.at[m])

        @pl.when(section < SECTIONS - 1)
        def _():
            arrived(features.at[m], layer_send.at[m])

        return carry

    lax.fori_loop(0, STEPS, drain, 0)


def shards(
    patches,
    vit_gain,
    vit_up,
    vit_down,
    project,
    text,
    image_counts,
    image_dest,
    layer_gain,
    layer_weight,
):
    vmem = pl.BlockSpec(memory_space=pltpu.VMEM)
    hbm = pl.BlockSpec(memory_space=pltpu.HBM)
    dma = pltpu.SemaphoreType.DMA
    hidden = vit_up.shape[1]
    outputs = pl.pallas_call(
        kernel,
        out_shape=jax.ShapeDtypeStruct((ROWS, WIDTH), BF16),
        in_specs=[hbm] * 10,
        out_specs=vmem,
        scratch_shapes=[
            pltpu.VMEM(patches.shape, BF16),
            pltpu.VMEM(vit_gain.shape, F32),
            pltpu.VMEM(image_counts.shape, jnp.int32),
            pltpu.VMEM(image_dest.shape, jnp.int32),
            pltpu.VMEM(layer_gain.shape, BF16),
            pltpu.VMEM((DV, hidden), BF16),
            pltpu.VMEM((hidden, DV), BF16),
            pltpu.VMEM((DV, WIDTH), BF16),
            pltpu.VMEM((ROWS, WIDTH), BF16),
            pltpu.VMEM((TP, WIDTH, WIDTH), BF16),
            pltpu.VMEM((TP, POOL, DV), BF16),
            pltpu.VMEM((COLS, TP, LANES), BF16),
            pltpu.VMEM((TP, TP, LANES), BF16),
            pltpu.VMEM((TP, DV), BF16),
            pltpu.VMEM((CAP, WIDTH), BF16),
            pltpu.VMEM((SECTIONS, CAP, WIDTH), BF16),
            pltpu.VMEM((ROWS, SECTIONS * CAP), BF16),
            pltpu.VMEM((ROWS, WIDTH), BF16),
            pltpu.VMEM((1, WIDTH), F32),
            pltpu.VMEM((TP, 1, WIDTH), F32),
            pltpu.VMEM((STEPS, TP, R, WIDTH), BF16),
            dma((9,)),
            dma,
            dma((5, TP)),
            dma((TP,)),
            dma((TP,)),
            dma((TP,)),
            dma((TP,)),
            dma((SECTIONS,)),
            dma((STEPS,)),
            dma((STEPS,)),
            dma((STEPS, TP)),
        ],
        compiler_params=pltpu.CompilerParams(
            collective_id=0, has_side_effects=True, vmem_limit_bytes=60 << 20
        ),
        cost_estimate=pl.CostEstimate(
            flops=2 * ROWS * D * WIDTH, bytes_accessed=12 << 20, transcendentals=0
        ),
        name="encoder_and_layers",
    )(
        patches,
        vit_gain,
        image_counts,
        image_dest,
        layer_gain,
        vit_up,
        vit_down,
        project,
        text,
        layer_weight[0],
    )
    return outputs.reshape(1, 8, ROWS // 8, WIDTH)


def solution(mesh):
    in_specs = (
        P(("section", "tp"), None),
        P(),
        P(None, "tp"),
        P("tp", None),
        P(None, "tp"),
        P(None, "tp"),
        P(),
        P(),
        P("section", "tp"),
        P("section", None, "tp"),
    )
    out_specs = P("section", None, None, "tp")
    return jax.shard_map(shards, mesh=mesh, in_specs=in_specs, out_specs=out_specs, check_vma=False)
```

```python
import functools

import jax
import jax.numpy as jnp
from jax import lax
from jax.experimental import pallas as pl
from jax.experimental.pallas import tpu as pltpu
from jax.sharding import PartitionSpec as P

MESH = pl.DeviceIdType.MESH
F32 = jnp.float32
BF16 = jnp.bfloat16

D = 8192
DV = 1664
POOL = 4
EPSILON = 1e-05
SIDE = 4
TP = SIDE * SIDE
SECTIONS = 16
ROWS = 256
CAP = 16
WIDTH = D // TP
LANES = 128
COLS = DV // LANES
R = 8
STEPS = ROWS // R
PAIRS = STEPS // 2
AHEAD = 2
BATCHES = 4


def hops(offset):
    return sum(min(o, SIDE - o) for o in offset)


OFFSETS = sorted(((a, b) for a in range(SIDE) for b in range(SIDE)), key=hops)
FAR_FIRST = list(reversed(list(enumerate(OFFSETS))))
CLASSES = [
    (lo, lo + sum(hops(o) == h for o in OFFSETS))
    for h, lo in [(hops(o), i) for i, o in enumerate(OFFSETS) if i == 0 or hops(o) != hops(OFFSETS[i - 1])]
]


def slot_at_target(offset):
    return OFFSETS.index(tuple((SIDE - o) % SIDE for o in offset))


def kernel(
    patches_in,
    vit_gain_in,
    counts_in,
    dest_in,
    layer_gain_in,
    vit_up,
    vit_down,
    project,
    text,
    weight,
    out,
    patches,
    vit_gain,
    counts,
    dest,
    layer_gain,
    up_v,
    down_v,
    project_v,
    text_v,
    weight_v,
    normed,
    partial,
    parts,
    pooled,
    embed_own,
    embeds,
    onehot,
    start,
    gain_own,
    gains,
    features,
    result,
    load_sem,
    weight_sem,
    phase_send,
    phase_recv,
    start_send,
    layer_send,
    feature_sem,
    out_sem,
):
    section = lax.axis_index("section")
    me = lax.axis_index("tp")
    x, y = me // SIDE, lax.rem(me, SIDE)
    targets = [
        lax.rem(x + offset[0], SIDE) * SIDE + lax.rem(y + offset[1], SIDE) for offset in OFFSETS
    ]
    peers = [(i, targets[i]) for i, _ in FAR_FIRST if i]

    barrier = pltpu.get_barrier_semaphore()

    def greet(to_section, to):
        pl.semaphore_signal(barrier, inc=1, device_id=(to_section, to), device_id_type=MESH)

    for _, to in peers:
        greet(section, to)

    @pl.when(section == 0)
    def _():
        for other in range(1, SECTIONS):
            greet(other, me)

    @pl.when(section > 0)
    def _():
        for i, _ in FAR_FIRST:
            greet(section - 1, targets[i])

    loads = [
        pltpu.make_async_copy(source, target, load_sem.at[i])
        for i, (source, target) in enumerate(
            (
                (patches_in, patches),
                (vit_gain_in, vit_gain),
                (layer_gain_in, layer_gain),
                (counts_in, counts),
                (dest_in, dest),
                (vit_up, up_v),
                (vit_down, down_v),
                (project, project_v),
                (text, text_v),
            )
        )
    ]
    for load in loads:
        load.start()
    for i in range(TP):
        pltpu.make_async_copy(
            weight.at[pl.ds(pl.multiple_of(targets[i] * WIDTH, WIDTH), WIDTH)],
            weight_v.at[i],
            weight_sem,
        ).start()

    for load in loads[:3]:
        load.wait()
    values = patches[...].astype(F32)
    centred = values - jnp.mean(values, axis=1, keepdims=True)
    spread = jnp.mean(centred * centred, axis=1, keepdims=True)
    normed[me] = (centred * lax.rsqrt(spread + EPSILON) * vit_gain[...][None]).astype(BF16)
    residual = jnp.mean(values, axis=0, keepdims=True)
    gain_own[...] = layer_gain[...].astype(F32)
    gains[0] = layer_gain[...].astype(F32)

    greeted = TP - 1 + jnp.where(section < SECTIONS - 1, TP, 0) + jnp.where(section > 0, 1, 0)
    pl.semaphore_wait(barrier, greeted)

    def send(source, target, recv_sem, to, sem, to_section=section):
        pltpu.make_async_remote_copy(
            src_ref=source,
            dst_ref=target,
            send_sem=sem,
            recv_sem=recv_sem,
            device_id=(to_section, to),
            device_id_type=MESH,
        ).start()

    def arrived(target, sem):
        pltpu.make_async_copy(target, target, sem).wait()

    for _, to in peers:
        send(normed.at[me], normed.at[me], phase_recv.at[0], to, phase_send.at[0])
    for i, to in peers:
        slot = slot_at_target(OFFSETS[i])
        send(gain_own, gains.at[slot], phase_recv.at[1], to, phase_send.at[1])

    loads[3].wait()
    loads[4].wait()

    @pl.when(section == 0)
    def _():
        square = (CAP, CAP)
        spots = lax.broadcasted_iota(jnp.int32, square, 1)
        groups = lax.broadcasted_iota(jnp.int32, square, 0)
        limits = jnp.sum(
            jnp.where(spots == groups, counts[...][None].astype(F32), 0.0), axis=1, keepdims=True
        )
        wanted = jnp.where(spots.astype(F32) < limits, dest[...].astype(F32), -1.0)
        flat = (CAP, SECTIONS * CAP)
        column = lax.broadcasted_iota(jnp.int32, flat, 1)
        line = lax.broadcasted_iota(jnp.int32, flat, 0)
        spread_out = jnp.dot(
            wanted.astype(BF16), (column % CAP == line).astype(BF16), preferred_element_type=F32
        )
        places = jnp.sum(jnp.where(column // CAP == line, spread_out, 0.0), axis=0, keepdims=True)
        rows = lax.broadcasted_iota(jnp.int32, (ROWS, SECTIONS * CAP), 0).astype(F32)
        onehot[...] = (rows == places).astype(BF16)

    loads[5].wait()
    loads[6].wait()
    arrived(normed.at[pl.ds(0, TP - 1)], phase_recv.at[0])
    whole = normed[...].reshape(TP * POOL, DV)
    hidden = jax.nn.gelu(
        jnp.dot(whole, up_v[...], preferred_element_type=F32), approximate=True
    ).astype(BF16)
    merge = lax.broadcasted_iota(jnp.int32, (TP, TP * POOL), 1) // POOL == lax.broadcasted_iota(
        jnp.int32, (TP, TP * POOL), 0
    )
    merged = jnp.dot(
        jnp.where(merge, 1.0 / POOL, 0.0).astype(BF16), hidden, preferred_element_type=F32
    )
    terms = jnp.dot(merged.astype(BF16), down_v[...], preferred_element_type=F32)
    mine = lax.broadcasted_iota(jnp.int32, (TP, DV), 0) == me
    terms = (terms + jnp.where(mine, residual, 0.0)).astype(BF16)
    for j in range(COLS):
        partial[j] = terms[:, j * LANES : (j + 1) * LANES]

    for i, to in peers:

        @pl.when(to < COLS)
        def _():
            send(partial.at[to], parts.at[me], phase_recv.at[2], to, phase_send.at[2])

    @pl.when(me < COLS)
    def _():
        parts[me] = partial[me]
        arrived(parts.at[pl.ds(0, TP - 1)], phase_recv.at[2])
        total = jnp.sum(parts[...].astype(F32), axis=0)
        block = pl.ds(pl.multiple_of(me * LANES, LANES), LANES)
        pooled[:, block] = total.astype(BF16)
        for _, to in peers:
            send(pooled.at[:, block], pooled.at[:, block], phase_recv.at[3], to, phase_send.at[3])
        arrived(pooled.at[:, pl.ds(0, (COLS - 1) * LANES)], phase_recv.at[3])

    @pl.when(me >= COLS)
    def _():
        arrived(pooled, phase_recv.at[3])

    loads[7].wait()
    embed = jnp.dot(pooled[...], project_v[...], preferred_element_type=F32).astype(BF16)

    @pl.when(section > 0)
    def _():
        embed_own[...] = embed
        send(embed_own, embeds.at[section], phase_recv.at[4], me, phase_send.at[4], 0)

    loads[8].wait()

    def spread_rows(p):
        two = pl.ds(2 * p, 2)
        features[two, 0] = start[two]
        for i, to in peers:
            slot = slot_at_target(OFFSETS[i])
            (c,) = [c for c, (lo, hi) in enumerate(CLASSES) if lo <= slot < hi]
            send(
                start.at[two],
                features.at[two, slot],
                feature_sem.at[2 * p, c],
                to,
                start_send.at[2 * p * BATCHES // STEPS],
            )

    @pl.when(section == 0)
    def _():
        embeds[0] = embed
        arrived(embeds.at[pl.ds(0, SECTIONS - 1)], phase_recv.at[4])
        for p in range(PAIRS):
            rows = slice(2 * R * p, 2 * R * (p + 1))
            placed = jnp.dot(
                onehot[rows, :],
                embeds[...].reshape(SECTIONS * CAP, WIDTH),
                preferred_element_type=F32,
            )
            first = text_v[rows, :].astype(F32) + placed
            start[2 * p : 2 * p + 2] = first.reshape(2, R, WIDTH).astype(BF16)
            if p < AHEAD:
                spread_rows(p)

    arrived(gains.at[pl.ds(0, TP - 1)], phase_recv.at[1])
    arrived(weight_v, weight_sem)

    def layer(m, wait):
        product = jnp.zeros((R, WIDTH), F32)
        squares = jnp.zeros((R, LANES), F32)
        for c, (lo, hi) in enumerate(CLASSES):
            wait(c, pl.ds(lo, hi - lo))
            for i in range(lo, hi):
                part = features[m, i].astype(F32)
                for at in range(0, WIDTH, LANES):
                    squares += part[:, at : at + LANES] * part[:, at : at + LANES]
                scaled = (part * gains[i]).astype(BF16)
                product += jnp.dot(scaled, weight_v[i], preferred_element_type=F32)
        scale = lax.rsqrt(jnp.sum(squares, axis=1, keepdims=True) / D + EPSILON)
        result[m] = (features[m, 0].astype(F32) + product * scale).astype(BF16)

    def hand_on(m):
        for i, offset in FAR_FIRST:
            slot = slot_at_target(offset)
            (c,) = [c for c, (lo, hi) in enumerate(CLASSES) if lo <= slot < hi]
            send(
                result.at[m],
                features.at[m, slot],
                feature_sem.at[m, c],
                targets[i],
                layer_send.at[m * BATCHES // STEPS],
                section + 1,
            )

    def store(p):
        two = pl.ds(2 * p, 2)
        pltpu.make_async_copy(result.at[two], out.at[two], out_sem).start()

    @pl.when(section == 0)
    def _():
        def pair(p, carry):
            @pl.when(p + AHEAD < PAIRS)
            def _():
                spread_rows(p + AHEAD)

            def wait(c, slots):
                if c:
                    arrived(features.at[pl.ds(2 * p, 2), slots], feature_sem.at[2 * p, c])

            layer(2 * p, wait)
            hand_on(2 * p)
            layer(2 * p + 1, lambda c, slots: None)
            hand_on(2 * p + 1)
            store(p)
            return carry

        lax.fori_loop(0, PAIRS, pair, 0)

    @pl.when(section > 0)
    def _():
        def pair(p, carry):
            for m in (2 * p, 2 * p + 1):
                layer(m, lambda c, slots: arrived(features.at[m, slots], feature_sem.at[m, c]))

                @pl.when(section < SECTIONS - 1)
                def _():
                    hand_on(m)

            store(p)
            return carry

        lax.fori_loop(0, PAIRS, pair, 0)

    arrived(normed.at[pl.ds(0, TP - 1)], phase_send.at[0])
    arrived(gains.at[pl.ds(0, TP - 1)], phase_send.at[1])

    @pl.when(me < COLS)
    def _():
        arrived(partial.at[pl.ds(0, COLS - 1)], phase_send.at[2])
        arrived(parts.at[pl.ds(0, TP - 1)], phase_send.at[3])

    @pl.when(me >= COLS)
    def _():
        arrived(partial, phase_send.at[2])

    @pl.when(section > 0)
    def _():
        arrived(embed_own, phase_send.at[4])

    many = STEPS // BATCHES

    @pl.when(section == 0)
    def _():
        for b in range(BATCHES):
            arrived(features.at[pl.ds(b * many, many), pl.ds(0, TP - 1)], start_send.at[b])

    @pl.when(section < SECTIONS - 1)
    def _():
        for b in range(BATCHES):
            arrived(features.at[pl.ds(b * many, many)], layer_send.at[b])

    arrived(result, out_sem)


def shards(
    patches,
    vit_gain,
    vit_up,
    vit_down,
    project,
    text,
    image_counts,
    image_dest,
    layer_gain,
    layer_weight,
):
    hbm = pl.BlockSpec(memory_space=pltpu.HBM)
    dma = pltpu.SemaphoreType.DMA
    hidden = vit_up.shape[1]
    outputs = pl.pallas_call(
        kernel,
        out_shape=jax.ShapeDtypeStruct((STEPS, R, WIDTH), BF16),
        in_specs=[hbm] * 10,
        out_specs=hbm,
        scratch_shapes=[
            pltpu.VMEM(patches.shape, BF16),
            pltpu.VMEM(vit_gain.shape, F32),
            pltpu.VMEM(image_counts.shape, jnp.int32),
            pltpu.VMEM(image_dest.shape, jnp.int32),
            pltpu.VMEM(layer_gain.shape, BF16),
            pltpu.VMEM((DV, hidden), BF16),
            pltpu.VMEM((hidden, DV), BF16),
            pltpu.VMEM((DV, WIDTH), BF16),
            pltpu.VMEM((ROWS, WIDTH), BF16),
            pltpu.VMEM((TP, WIDTH, WIDTH), BF16),
            pltpu.VMEM((TP, POOL, DV), BF16),
            pltpu.VMEM((COLS, TP, LANES), BF16),
            pltpu.VMEM((TP, TP, LANES), BF16),
            pltpu.VMEM((TP, DV), BF16),
            pltpu.VMEM((CAP, WIDTH), BF16),
            pltpu.VMEM((SECTIONS, CAP, WIDTH), BF16),
            pltpu.VMEM((ROWS, SECTIONS * CAP), BF16),
            pltpu.VMEM((STEPS, R, WIDTH), BF16),
            pltpu.VMEM((1, WIDTH), F32),
            pltpu.VMEM((TP, 1, WIDTH), F32),
            pltpu.VMEM((STEPS, TP, R, WIDTH), BF16),
            pltpu.VMEM((STEPS, R, WIDTH), BF16),
            dma((9,)),
            dma,
            dma((5,)),
            dma((5,)),
            dma((BATCHES,)),
            dma((BATCHES,)),
            dma((STEPS, len(CLASSES))),
            dma,
        ],
        compiler_params=pltpu.CompilerParams(
            collective_id=0, has_side_effects=True, vmem_limit_bytes=60 << 20
        ),
        cost_estimate=pl.CostEstimate(
            flops=2 * ROWS * D * WIDTH, bytes_accessed=12 << 20, transcendentals=0
        ),
        name="encoder_and_layers",
    )(
        patches,
        vit_gain,
        image_counts,
        image_dest,
        layer_gain,
        vit_up,
        vit_down,
        project,
        text,
        layer_weight[0],
    )
    return outputs.reshape(1, 8, ROWS // 8, WIDTH)


def solution(mesh):
    in_specs = (
        P(("section", "tp"), None),
        P(),
        P(None, "tp"),
        P("tp", None),
        P(None, "tp"),
        P(None, "tp"),
        P(),
        P(),
        P("section", "tp"),
        P("section", None, "tp"),
    )
    out_specs = P("section", None, None, "tp")
    return jax.shard_map(shards, mesh=mesh, in_specs=in_specs, out_specs=out_specs, check_vma=False)
```

```python
import functools

import jax
import jax.numpy as jnp
from jax import lax
from jax.experimental import pallas as pl
from jax.experimental.pallas import tpu as pltpu
from jax.sharding import PartitionSpec as P

MESH = pl.DeviceIdType.MESH
F32 = jnp.float32
BF16 = jnp.bfloat16

D = 8192
DV = 1664
POOL = 4
EPSILON = 1e-05
SIDE = 4
TP = SIDE * SIDE
SECTIONS = 16
ROWS = 256
CAP = 16
WIDTH = D // TP
LANES = 128
COLS = DV // LANES
R = 8
STEPS = ROWS // R
PAIRS = STEPS // 2
HALF = TP // 2
BATCHES = 4


def hops(offset):
    return sum(min(o, SIDE - o) for o in offset)


OFFSETS = sorted(((a, b) for a in range(SIDE) for b in range(SIDE)), key=hops)
FAR_FIRST = list(reversed(list(enumerate(OFFSETS))))
CLASSES = [
    (lo, lo + sum(hops(o) == h for o in OFFSETS))
    for h, lo in [(hops(o), i) for i, o in enumerate(OFFSETS) if i == 0 or hops(o) != hops(OFFSETS[i - 1])]
]


def slot_at_target(offset):
    return OFFSETS.index(tuple((SIDE - o) % SIDE for o in offset))


def kernel(
    patches_in,
    vit_gain_in,
    counts_in,
    dest_in,
    layer_gain_in,
    vit_up,
    vit_down,
    project,
    text,
    weight,
    out,
    patches,
    vit_gain,
    counts,
    dest,
    layer_gain,
    up_v,
    down_v,
    project_v,
    text_v,
    weight_v,
    normed,
    partial,
    parts,
    pooled,
    start,
    onehot,
    gain_own,
    gains,
    features,
    result,
    ordered,
    load_sem,
    weight_sem,
    phase_send,
    phase_recv,
    start_send,
    layer_send,
    feature_sem,
    out_sem,
    token,
):
    section = lax.axis_index("section")
    me = lax.axis_index("tp")
    x, y = me // SIDE, lax.rem(me, SIDE)
    targets = [
        lax.rem(x + offset[0], SIDE) * SIDE + lax.rem(y + offset[1], SIDE) for offset in OFFSETS
    ]
    peers = [(i, targets[i]) for i, _ in FAR_FIRST if i]

    barrier = pltpu.get_barrier_semaphore()

    def greet(to_section, to):
        pl.semaphore_signal(barrier, inc=1, device_id=(to_section, to), device_id_type=MESH)

    for _, to in peers:
        greet(section, to)

    @pl.when(section > 0)
    def _():
        for i, _ in FAR_FIRST:
            greet(section - 1, targets[i])

    loads = [
        pltpu.make_async_copy(source, target, load_sem.at[i])
        for i, (source, target) in enumerate(
            (
                (patches_in, patches),
                (vit_gain_in, vit_gain),
                (layer_gain_in, layer_gain),
                (counts_in, counts),
                (dest_in, dest),
                (vit_up, up_v),
                (vit_down, down_v),
                (project, project_v),
                (text, text_v),
            )
        )
    ]
    for load in loads:
        load.start()
    for i in range(TP):
        pltpu.make_async_copy(
            weight.at[pl.ds(pl.multiple_of(targets[i] * WIDTH, WIDTH), WIDTH)],
            weight_v.at[i],
            weight_sem,
        ).start()

    for load in loads[:3]:
        load.wait()
    values = patches[...].astype(F32)
    centred = values - jnp.mean(values, axis=1, keepdims=True)
    spread = jnp.mean(centred * centred, axis=1, keepdims=True)
    normed[me] = (centred * lax.rsqrt(spread + EPSILON) * vit_gain[...][None]).astype(BF16)
    residual = jnp.mean(values, axis=0, keepdims=True)
    gain_own[...] = layer_gain[...].astype(F32)
    gains[0] = layer_gain[...].astype(F32)

    pl.semaphore_wait(barrier, TP - 1 + jnp.where(section < SECTIONS - 1, TP, 0))

    def send(source, target, recv_sem, to, sem, to_section=section):
        pltpu.make_async_remote_copy(
            src_ref=source,
            dst_ref=target,
            send_sem=sem,
            recv_sem=recv_sem,
            device_id=(to_section, to),
            device_id_type=MESH,
        ).start()

    def arrived(target, sem):
        pltpu.make_async_copy(target, target, sem).wait()

    for _, to in peers:
        send(normed.at[me], normed.at[me], phase_recv.at[0], to, phase_send.at[0])
    for i, to in peers:
        slot = slot_at_target(OFFSETS[i])
        send(gain_own, gains.at[slot], phase_recv.at[1], to, phase_send.at[1])

    loads[3].wait()
    loads[4].wait()
    loads[8].wait()
    square = (CAP, CAP)
    lane = lax.broadcasted_iota(jnp.int32, square, 1)
    line = lax.broadcasted_iota(jnp.int32, square, 0)
    places = dest[...].astype(F32)
    limit = jnp.sum(
        jnp.where(lane[:1] == section, counts[...][None].astype(F32), 0.0), axis=1, keepdims=True
    )
    live = lax.broadcasted_iota(jnp.int32, (CAP, 1), 0).astype(F32) < limit
    own_place = jnp.sum(jnp.where(line == section, places, 0.0), axis=0, keepdims=True)
    own_place = jnp.sum(jnp.where(line == lane, own_place, 0.0), axis=1, keepdims=True)
    position = lax.broadcasted_iota(jnp.int32, (CAP, ROWS), 1).astype(F32)
    own_text = jnp.dot(
        (position == own_place).astype(BF16), text_v[...], preferred_element_type=F32
    )

    loads[5].wait()
    loads[6].wait()
    arrived(normed.at[pl.ds(0, TP - 1)], phase_recv.at[0])
    whole = normed[...].reshape(TP * POOL, DV)
    hidden = jax.nn.gelu(
        jnp.dot(whole, up_v[...], preferred_element_type=F32), approximate=True
    ).astype(BF16)
    merge = lax.broadcasted_iota(jnp.int32, (TP, TP * POOL), 1) // POOL == lax.broadcasted_iota(
        jnp.int32, (TP, TP * POOL), 0
    )
    merged = jnp.dot(
        jnp.where(merge, 1.0 / POOL, 0.0).astype(BF16), hidden, preferred_element_type=F32
    )
    terms = jnp.dot(merged.astype(BF16), down_v[...], preferred_element_type=F32)
    mine = lax.broadcasted_iota(jnp.int32, (TP, DV), 0) == me
    terms = (terms + jnp.where(mine, residual, 0.0)).astype(BF16)
    for j in range(COLS):
        partial[j] = terms[:, j * LANES : (j + 1) * LANES]

    for i, to in peers:

        @pl.when(to < COLS)
        def _():
            send(partial.at[to], parts.at[me], phase_recv.at[2], to, phase_send.at[2])

    @pl.when(me < COLS)
    def _():
        parts[me] = partial[me]
        arrived(parts.at[pl.ds(0, TP - 1)], phase_recv.at[2])
        total = jnp.sum(parts[...].astype(F32), axis=0)
        block = pl.ds(pl.multiple_of(me * LANES, LANES), LANES)
        pooled[:, block] = total.astype(BF16)
        for _, to in peers:
            send(pooled.at[:, block], pooled.at[:, block], phase_recv.at[3], to, phase_send.at[3])
        arrived(pooled.at[:, pl.ds(0, (COLS - 1) * LANES)], phase_recv.at[3])

    @pl.when(me >= COLS)
    def _():
        arrived(pooled, phase_recv.at[3])

    loads[7].wait()
    embed = jnp.dot(pooled[...], project_v[...], preferred_element_type=F32).astype(BF16)

    start[...] = (
        (own_text + jnp.where(live, embed.astype(F32), 0.0)).astype(BF16).reshape(2, R, WIDTH)
    )
    own_pair = pl.ds(2 * section, 2)

    def class_of(slot):
        (c,) = [c for c, (lo, hi) in enumerate(CLASSES) if lo <= slot < hi]
        return c

    def send_start(count, which):
        for n, (i, offset) in enumerate(FAR_FIRST[:count]):
            slot = slot_at_target(offset)
            send(
                start,
                features.at[own_pair, slot],
                feature_sem.at[2 * section, class_of(slot)],
                targets[i],
                start_send.at[which(n)],
                0,
            )

    def pass_token():
        pl.semaphore_signal(token, inc=1, device_id=(section + 1, me), device_id_type=MESH)

    @pl.when(section == 0)
    def _():
        features[pl.ds(0, 2), 0] = start[...]
        send_start(TP - 1, lambda n: 0)
        pass_token()

    @pl.when(section > 0)
    def _():
        pl.semaphore_wait(token, 1)
        send_start(TP, lambda n: n // HALF)
        arrived(features.at[pl.ds(0, 2), pl.ds(0, HALF)], start_send.at[0])

        @pl.when(section < SECTIONS - 1)
        def _():
            pass_token()

    flat = (CAP, ROWS)
    column = lax.broadcasted_iota(jnp.int32, flat, 1)
    line = lax.broadcasted_iota(jnp.int32, flat, 0)
    spread_out = jnp.dot(
        places.astype(BF16), (column % CAP == line).astype(BF16), preferred_element_type=F32
    )
    places = jnp.sum(jnp.where(column // CAP == line, spread_out, 0.0), axis=0, keepdims=True)
    position = lax.broadcasted_iota(jnp.int32, (ROWS, ROWS), 0).astype(F32)
    onehot[...] = (position == places).astype(BF16)

    arrived(gains.at[pl.ds(0, TP - 1)], phase_recv.at[1])
    arrived(weight_v, weight_sem)

    def layer(m, wait):
        product = jnp.zeros((R, WIDTH), F32)
        squares = jnp.zeros((R, LANES), F32)
        for c, (lo, hi) in enumerate(CLASSES):
            wait(c, pl.ds(lo, hi - lo))
            for i in range(lo, hi):
                part = features[m, i].astype(F32)
                for at in range(0, WIDTH, LANES):
                    squares += part[:, at : at + LANES] * part[:, at : at + LANES]
                scaled = (part * gains[i]).astype(BF16)
                product += jnp.dot(scaled, weight_v[i], preferred_element_type=F32)
        scale = lax.rsqrt(jnp.sum(squares, axis=1, keepdims=True) / D + EPSILON)
        result[m] = (features[m, 0].astype(F32) + product * scale).astype(BF16)

    def hand_on(m):
        for i, offset in FAR_FIRST:
            slot = slot_at_target(offset)
            send(
                result.at[m],
                features.at[m, slot],
                feature_sem.at[m, class_of(slot)],
                targets[i],
                layer_send.at[m * BATCHES // STEPS],
                section + 1,
            )

    @pl.when(section == 0)
    def _():
        def pair(p, carry):
            def wait(c, slots):
                def both():
                    arrived(features.at[pl.ds(2 * p, 2), slots], feature_sem.at[2 * p, c])

                if c:
                    both()
                else:
                    pl.when(p > 0)(both)

            layer(2 * p, wait)
            hand_on(2 * p)
            layer(2 * p + 1, lambda c, slots: None)
            hand_on(2 * p + 1)
            return carry

        lax.fori_loop(0, PAIRS, pair, 0)

    @pl.when(section > 0)
    def _():
        def pair(p, carry):
            for m in (2 * p, 2 * p + 1):
                layer(m, lambda c, slots: arrived(features.at[m, slots], feature_sem.at[m, c]))

                @pl.when(section < SECTIONS - 1)
                def _():
                    hand_on(m)

            return carry

        lax.fori_loop(0, PAIRS, pair, 0)

    pieces = []
    for b in range(BATCHES):
        rows = slice(b * ROWS // BATCHES, (b + 1) * ROWS // BATCHES)
        ordered[rows, :] = jnp.dot(
            onehot[rows, :], result[...].reshape(ROWS, WIDTH), preferred_element_type=F32
        ).astype(BF16)
        pieces.append(pltpu.make_async_copy(ordered.at[rows, :], out.at[rows, :], out_sem.at[b]))
        pieces[b].start()

    arrived(normed.at[pl.ds(0, TP - 1)], phase_send.at[0])
    arrived(gains.at[pl.ds(0, TP - 1)], phase_send.at[1])

    @pl.when(me < COLS)
    def _():
        arrived(partial.at[pl.ds(0, COLS - 1)], phase_send.at[2])
        arrived(parts.at[pl.ds(0, TP - 1)], phase_send.at[3])

    @pl.when(me >= COLS)
    def _():
        arrived(partial, phase_send.at[2])

    many = STEPS // BATCHES

    @pl.when(section == 0)
    def _():
        arrived(features.at[pl.ds(0, 2), pl.ds(0, TP - 1)], start_send.at[0])

    @pl.when(section > 0)
    def _():
        arrived(features.at[pl.ds(0, 2), pl.ds(0, HALF)], start_send.at[1])

    @pl.when(section < SECTIONS - 1)
    def _():
        for b in range(BATCHES):
            arrived(features.at[pl.ds(b * many, many)], layer_send.at[b])

    for piece in pieces:
        piece.wait()


def shards(
    patches,
    vit_gain,
    vit_up,
    vit_down,
    project,
    text,
    image_counts,
    image_dest,
    layer_gain,
    layer_weight,
):
    hbm = pl.BlockSpec(memory_space=pltpu.HBM)
    dma = pltpu.SemaphoreType.DMA
    hidden = vit_up.shape[1]
    outputs = pl.pallas_call(
        kernel,
        out_shape=jax.ShapeDtypeStruct((ROWS, WIDTH), BF16),
        in_specs=[hbm] * 10,
        out_specs=hbm,
        scratch_shapes=[
            pltpu.VMEM(patches.shape, BF16),
            pltpu.VMEM(vit_gain.shape, F32),
            pltpu.VMEM(image_counts.shape, jnp.int32),
            pltpu.VMEM(image_dest.shape, jnp.int32),
            pltpu.VMEM(layer_gain.shape, BF16),
            pltpu.VMEM((DV, hidden), BF16),
            pltpu.VMEM((hidden, DV), BF16),
            pltpu.VMEM((DV, WIDTH), BF16),
            pltpu.VMEM((ROWS, WIDTH), BF16),
            pltpu.VMEM((TP, WIDTH, WIDTH), BF16),
            pltpu.VMEM((TP, POOL, DV), BF16),
            pltpu.VMEM((COLS, TP, LANES), BF16),
            pltpu.VMEM((TP, TP, LANES), BF16),
            pltpu.VMEM((TP, DV), BF16),
            pltpu.VMEM((2, R, WIDTH), BF16),
            pltpu.VMEM((ROWS, ROWS), BF16),
            pltpu.VMEM((1, WIDTH), F32),
            pltpu.VMEM((TP, 1, WIDTH), F32),
            pltpu.VMEM((STEPS, TP, R, WIDTH), BF16),
            pltpu.VMEM((STEPS, R, WIDTH), BF16),
            pltpu.VMEM((ROWS, WIDTH), BF16),
            dma((9,)),
            dma,
            dma((4,)),
            dma((4,)),
            dma((2,)),
            dma((BATCHES,)),
            dma((STEPS, len(CLASSES))),
            dma((BATCHES,)),
            pltpu.SemaphoreType.REGULAR,
        ],
        compiler_params=pltpu.CompilerParams(
            collective_id=0, has_side_effects=True, vmem_limit_bytes=60 << 20
        ),
        cost_estimate=pl.CostEstimate(
            flops=2 * ROWS * D * WIDTH, bytes_accessed=12 << 20, transcendentals=0
        ),
        name="encoder_and_layers",
    )(
        patches,
        vit_gain,
        image_counts,
        image_dest,
        layer_gain,
        vit_up,
        vit_down,
        project,
        text,
        layer_weight[0],
    )
    return outputs.reshape(1, 8, ROWS // 8, WIDTH)


def solution(mesh):
    in_specs = (
        P(("section", "tp"), None),
        P(),
        P(None, "tp"),
        P("tp", None),
        P(None, "tp"),
        P(None, "tp"),
        P(),
        P(),
        P("section", "tp"),
        P("section", None, "tp"),
    )
    out_specs = P("section", None, None, "tp")
    return jax.shard_map(shards, mesh=mesh, in_specs=in_specs, out_specs=out_specs, check_vma=False)
```

```python
import functools

import jax
import jax.numpy as jnp
from jax import lax
from jax.experimental import pallas as pl
from jax.experimental.pallas import tpu as pltpu
from jax.sharding import PartitionSpec as P

MESH = pl.DeviceIdType.MESH
F32 = jnp.float32
BF16 = jnp.bfloat16

D = 8192
DV = 1664
POOL = 4
EPSILON = 1e-05
SIDE = 4
TP = SIDE * SIDE
SECTIONS = 16
ROWS = 256
CAP = 16
WIDTH = D // TP
LANES = 128
COLS = DV // LANES
R = 8
STEPS = ROWS // R
PAIRS = STEPS // 2
HALF = TP // 2
BATCHES = 4


def hops(offset):
    return sum(min(o, SIDE - o) for o in offset)


OFFSETS = sorted(((a, b) for a in range(SIDE) for b in range(SIDE)), key=hops)
FAR_FIRST = list(reversed(list(enumerate(OFFSETS))))
CLASSES = [
    (lo, lo + sum(hops(o) == h for o in OFFSETS))
    for h, lo in [(hops(o), i) for i, o in enumerate(OFFSETS) if i == 0 or hops(o) != hops(OFFSETS[i - 1])]
]


def slot_at_target(offset):
    return OFFSETS.index(tuple((SIDE - o) % SIDE for o in offset))


def kernel(
    patches_in,
    vit_gain_in,
    counts_in,
    dest_in,
    layer_gain_in,
    vit_up,
    vit_down,
    project,
    text,
    weight,
    out,
    patches,
    vit_gain,
    counts,
    dest,
    layer_gain,
    up_v,
    down_v,
    project_v,
    text_v,
    weight_v,
    normed,
    partial,
    parts,
    pooled,
    start,
    gain_own,
    gains,
    features,
    result,
    load_sem,
    weight_sem,
    phase_send,
    phase_recv,
    start_send,
    layer_send,
    feature_sem,
    out_sem,
    token,
):
    section = lax.axis_index("section")
    me = lax.axis_index("tp")
    x, y = me // SIDE, lax.rem(me, SIDE)
    targets = [
        lax.rem(x + offset[0], SIDE) * SIDE + lax.rem(y + offset[1], SIDE) for offset in OFFSETS
    ]
    peers = [(i, targets[i]) for i, _ in FAR_FIRST if i]

    barrier = pltpu.get_barrier_semaphore()

    def greet(to_section, to):
        pl.semaphore_signal(barrier, inc=1, device_id=(to_section, to), device_id_type=MESH)

    for _, to in peers:
        greet(section, to)

    @pl.when(section > 0)
    def _():
        for i, _ in FAR_FIRST:
            greet(section - 1, targets[i])

    loads = [
        pltpu.make_async_copy(source, target, load_sem.at[i])
        for i, (source, target) in enumerate(
            (
                (patches_in, patches),
                (vit_gain_in, vit_gain),
                (layer_gain_in, layer_gain),
                (counts_in, counts),
                (dest_in, dest),
                (vit_up, up_v),
                (vit_down, down_v),
                (project, project_v),
                (text, text_v),
            )
        )
    ]
    for load in loads:
        load.start()
    for i in range(TP):
        pltpu.make_async_copy(
            weight.at[pl.ds(pl.multiple_of(targets[i] * WIDTH, WIDTH), WIDTH)],
            weight_v.at[i],
            weight_sem,
        ).start()

    for load in loads[:3]:
        load.wait()
    values = patches[...].astype(F32)
    centred = values - jnp.mean(values, axis=1, keepdims=True)
    spread = jnp.mean(centred * centred, axis=1, keepdims=True)
    normed[me] = (centred * lax.rsqrt(spread + EPSILON) * vit_gain[...][None]).astype(BF16)
    residual = jnp.mean(values, axis=0, keepdims=True)
    gain_own[...] = layer_gain[...].astype(F32)
    gains[0] = layer_gain[...].astype(F32)

    pl.semaphore_wait(barrier, TP - 1 + jnp.where(section < SECTIONS - 1, TP, 0))

    def send(source, target, recv_sem, to, sem, to_section=section):
        pltpu.make_async_remote_copy(
            src_ref=source,
            dst_ref=target,
            send_sem=sem,
            recv_sem=recv_sem,
            device_id=(to_section, to),
            device_id_type=MESH,
        ).start()

    def arrived(target, sem):
        pltpu.make_async_copy(target, target, sem).wait()

    for _, to in peers:
        send(normed.at[me], normed.at[me], phase_recv.at[0], to, phase_send.at[0])
    for i, to in peers:
        slot = slot_at_target(OFFSETS[i])
        send(gain_own, gains.at[slot], phase_recv.at[1], to, phase_send.at[1])

    loads[3].wait()
    loads[4].wait()
    loads[8].wait()
    square = (CAP, CAP)
    lane = lax.broadcasted_iota(jnp.int32, square, 1)
    line = lax.broadcasted_iota(jnp.int32, square, 0)
    places = dest[...].astype(F32)
    limit = jnp.sum(
        jnp.where(lane[:1] == section, counts[...][None].astype(F32), 0.0), axis=1, keepdims=True
    )
    live = lax.broadcasted_iota(jnp.int32, (CAP, 1), 0).astype(F32) < limit
    own_place = jnp.sum(jnp.where(line == section, places, 0.0), axis=0, keepdims=True)
    own_place = jnp.sum(jnp.where(line == lane, own_place, 0.0), axis=1, keepdims=True)
    position = lax.broadcasted_iota(jnp.int32, (CAP, ROWS), 1).astype(F32)
    own_text = jnp.dot(
        (position == own_place).astype(BF16), text_v[...], preferred_element_type=F32
    )

    loads[5].wait()
    loads[6].wait()
    arrived(normed.at[pl.ds(0, TP - 1)], phase_recv.at[0])
    whole = normed[...].reshape(TP * POOL, DV)
    hidden = jax.nn.gelu(
        jnp.dot(whole, up_v[...], preferred_element_type=F32), approximate=True
    ).astype(BF16)
    merge = lax.broadcasted_iota(jnp.int32, (TP, TP * POOL), 1) // POOL == lax.broadcasted_iota(
        jnp.int32, (TP, TP * POOL), 0
    )
    merged = jnp.dot(
        jnp.where(merge, 1.0 / POOL, 0.0).astype(BF16), hidden, preferred_element_type=F32
    )
    terms = jnp.dot(merged.astype(BF16), down_v[...], preferred_element_type=F32)
    mine = lax.broadcasted_iota(jnp.int32, (TP, DV), 0) == me
    terms = (terms + jnp.where(mine, residual, 0.0)).astype(BF16)
    for j in range(COLS):
        partial[j] = terms[:, j * LANES : (j + 1) * LANES]

    for i, to in peers:

        @pl.when(to < COLS)
        def _():
            send(partial.at[to], parts.at[me], phase_recv.at[2], to, phase_send.at[2])

    @pl.when(me < COLS)
    def _():
        parts[me] = partial[me]
        arrived(parts.at[pl.ds(0, TP - 1)], phase_recv.at[2])
        total = jnp.sum(parts[...].astype(F32), axis=0)
        block = pl.ds(pl.multiple_of(me * LANES, LANES), LANES)
        pooled[:, block] = total.astype(BF16)
        for _, to in peers:
            send(pooled.at[:, block], pooled.at[:, block], phase_recv.at[3], to, phase_send.at[3])
        arrived(pooled.at[:, pl.ds(0, (COLS - 1) * LANES)], phase_recv.at[3])

    @pl.when(me >= COLS)
    def _():
        arrived(pooled, phase_recv.at[3])

    loads[7].wait()
    embed = jnp.dot(pooled[...], project_v[...], preferred_element_type=F32).astype(BF16)

    start[...] = (
        (own_text + jnp.where(live, embed.astype(F32), 0.0)).astype(BF16).reshape(2, R, WIDTH)
    )
    own_pair = pl.ds(2 * section, 2)

    def class_of(slot):
        (c,) = [c for c, (lo, hi) in enumerate(CLASSES) if lo <= slot < hi]
        return c

    def send_start(count, which):
        for n, (i, offset) in enumerate(FAR_FIRST[:count]):
            slot = slot_at_target(offset)
            send(
                start,
                features.at[own_pair, slot],
                feature_sem.at[2 * section, class_of(slot)],
                targets[i],
                start_send.at[which(n)],
                0,
            )

    def pass_token():
        pl.semaphore_signal(token, inc=1, device_id=(section + 1, me), device_id_type=MESH)

    @pl.when(section == 0)
    def _():
        features[pl.ds(0, 2), 0] = start[...]
        send_start(TP - 1, lambda n: 0)
        pass_token()

    @pl.when(section > 0)
    def _():
        pl.semaphore_wait(token, 1)
        send_start(TP, lambda n: n // HALF)
        arrived(features.at[pl.ds(0, 2), pl.ds(0, HALF)], start_send.at[0])

        @pl.when(section < SECTIONS - 1)
        def _():
            pass_token()

    arrived(gains.at[pl.ds(0, TP - 1)], phase_recv.at[1])
    arrived(weight_v, weight_sem)

    def layer(m, wait):
        product = jnp.zeros((R, WIDTH), F32)
        squares = jnp.zeros((R, LANES), F32)
        for c, (lo, hi) in enumerate(CLASSES):
            wait(c, pl.ds(lo, hi - lo))
            for i in range(lo, hi):
                part = features[m, i].astype(F32)
                for at in range(0, WIDTH, LANES):
                    squares += part[:, at : at + LANES] * part[:, at : at + LANES]
                scaled = (part * gains[i]).astype(BF16)
                product += jnp.dot(scaled, weight_v[i], preferred_element_type=F32)
        scale = lax.rsqrt(jnp.sum(squares, axis=1, keepdims=True) / D + EPSILON)
        result[m] = (features[m, 0].astype(F32) + product * scale).astype(BF16)

    def hand_on(m):
        for i, offset in FAR_FIRST:
            slot = slot_at_target(offset)
            send(
                result.at[m],
                features.at[m, slot],
                feature_sem.at[m, class_of(slot)],
                targets[i],
                layer_send.at[m * BATCHES // STEPS],
                section + 1,
            )

    def store(p):
        two = pl.ds(2 * p, 2)
        pltpu.make_async_copy(result.at[two], out.at[two], out_sem.at[0]).start()

    @pl.when(section == 0)
    def _():
        def pair(p, carry):
            def wait(c, slots):
                def both():
                    arrived(features.at[pl.ds(2 * p, 2), slots], feature_sem.at[2 * p, c])

                if c:
                    both()
                else:
                    pl.when(p > 0)(both)

            layer(2 * p, wait)
            hand_on(2 * p)
            layer(2 * p + 1, lambda c, slots: None)
            hand_on(2 * p + 1)
            store(p)
            return carry

        lax.fori_loop(0, PAIRS, pair, 0)

    @pl.when(section > 0)
    def _():
        def pair(p, carry):
            for m in (2 * p, 2 * p + 1):
                layer(m, lambda c, slots: arrived(features.at[m, slots], feature_sem.at[m, c]))

                @pl.when(section < SECTIONS - 1)
                def _():
                    hand_on(m)

            store(p)
            return carry

        lax.fori_loop(0, PAIRS, pair, 0)

    arrived(normed.at[pl.ds(0, TP - 1)], phase_send.at[0])
    arrived(gains.at[pl.ds(0, TP - 1)], phase_send.at[1])

    @pl.when(me < COLS)
    def _():
        arrived(partial.at[pl.ds(0, COLS - 1)], phase_send.at[2])
        arrived(parts.at[pl.ds(0, TP - 1)], phase_send.at[3])

    @pl.when(me >= COLS)
    def _():
        arrived(partial, phase_send.at[2])

    many = STEPS // BATCHES

    @pl.when(section == 0)
    def _():
        arrived(features.at[pl.ds(0, 2), pl.ds(0, TP - 1)], start_send.at[0])

    @pl.when(section > 0)
    def _():
        arrived(features.at[pl.ds(0, 2), pl.ds(0, HALF)], start_send.at[1])

    @pl.when(section < SECTIONS - 1)
    def _():
        for b in range(BATCHES):
            arrived(features.at[pl.ds(b * many, many)], layer_send.at[b])

    arrived(result, out_sem.at[0])


def shards(
    patches,
    vit_gain,
    vit_up,
    vit_down,
    project,
    text,
    image_counts,
    image_dest,
    layer_gain,
    layer_weight,
):
    hbm = pl.BlockSpec(memory_space=pltpu.HBM)
    dma = pltpu.SemaphoreType.DMA
    hidden = vit_up.shape[1]
    outputs = pl.pallas_call(
        kernel,
        out_shape=jax.ShapeDtypeStruct((STEPS, R, WIDTH), BF16),
        in_specs=[hbm] * 10,
        out_specs=hbm,
        scratch_shapes=[
            pltpu.VMEM(patches.shape, BF16),
            pltpu.VMEM(vit_gain.shape, F32),
            pltpu.VMEM(image_counts.shape, jnp.int32),
            pltpu.VMEM(image_dest.shape, jnp.int32),
            pltpu.VMEM(layer_gain.shape, BF16),
            pltpu.VMEM((DV, hidden), BF16),
            pltpu.VMEM((hidden, DV), BF16),
            pltpu.VMEM((DV, WIDTH), BF16),
            pltpu.VMEM((ROWS, WIDTH), BF16),
            pltpu.VMEM((TP, WIDTH, WIDTH), BF16),
            pltpu.VMEM((TP, POOL, DV), BF16),
            pltpu.VMEM((COLS, TP, LANES), BF16),
            pltpu.VMEM((TP, TP, LANES), BF16),
            pltpu.VMEM((TP, DV), BF16),
            pltpu.VMEM((2, R, WIDTH), BF16),
            pltpu.VMEM((1, WIDTH), F32),
            pltpu.VMEM((TP, 1, WIDTH), F32),
            pltpu.VMEM((STEPS, TP, R, WIDTH), BF16),
            pltpu.VMEM((STEPS, R, WIDTH), BF16),
            dma((9,)),
            dma,
            dma((4,)),
            dma((4,)),
            dma((2,)),
            dma((BATCHES,)),
            dma((STEPS, len(CLASSES))),
            dma((BATCHES,)),
            pltpu.SemaphoreType.REGULAR,
        ],
        compiler_params=pltpu.CompilerParams(
            collective_id=0, has_side_effects=True, vmem_limit_bytes=60 << 20
        ),
        cost_estimate=pl.CostEstimate(
            flops=2 * ROWS * D * WIDTH, bytes_accessed=12 << 20, transcendentals=0
        ),
        name="encoder_and_layers",
    )(
        patches,
        vit_gain,
        image_counts,
        image_dest,
        layer_gain,
        vit_up,
        vit_down,
        project,
        text,
        layer_weight[0],
    )
    slots = outputs.reshape(SECTIONS, CAP, WIDTH)
    onehot = (image_dest[:, :, None] == jnp.arange(ROWS, dtype=jnp.int32)).astype(BF16)
    ordered = lax.dot_general(
        onehot, slots, (((0, 1), (0, 1)), ((), ())), preferred_element_type=F32
    )
    return ordered.astype(BF16).reshape(1, 8, ROWS // 8, WIDTH)


def solution(mesh):
    in_specs = (
        P(("section", "tp"), None),
        P(),
        P(None, "tp"),
        P("tp", None),
        P(None, "tp"),
        P(None, "tp"),
        P(),
        P(),
        P("section", "tp"),
        P("section", None, "tp"),
    )
    out_specs = P("section", None, None, "tp")
    return jax.shard_map(shards, mesh=mesh, in_specs=in_specs, out_specs=out_specs, check_vma=False)
```

```python
import functools

import jax
import jax.numpy as jnp
from jax import lax
from jax.experimental import pallas as pl
from jax.experimental.pallas import tpu as pltpu
from jax.sharding import PartitionSpec as P

MESH = pl.DeviceIdType.MESH
F32 = jnp.float32
BF16 = jnp.bfloat16

D = 8192
DV = 1664
POOL = 4
EPSILON = 1e-05
SIDE = 4
TP = SIDE * SIDE
SECTIONS = 16
ROWS = 256
CAP = 16
WIDTH = D // TP
LANES = 128
COLS = DV // LANES
R = 8
STEPS = ROWS // R
PAIRS = STEPS // 2
BATCHES = 4


def hops(offset):
    return sum(min(o, SIDE - o) for o in offset)


OFFSETS = sorted(((a, b) for a in range(SIDE) for b in range(SIDE)), key=hops)
FAR_FIRST = list(reversed(list(enumerate(OFFSETS))))
CLASSES = [
    (lo, lo + sum(hops(o) == h for o in OFFSETS))
    for h, lo in [(hops(o), i) for i, o in enumerate(OFFSETS) if i == 0 or hops(o) != hops(OFFSETS[i - 1])]
]


def slot_at_target(offset):
    return OFFSETS.index(tuple((SIDE - o) % SIDE for o in offset))


def kernel(
    patches_in,
    vit_gain_in,
    counts_in,
    dest_in,
    layer_gain_in,
    vit_up,
    vit_down,
    project,
    text,
    weight,
    out,
    patches,
    vit_gain,
    counts,
    dest,
    layer_gain,
    up_v,
    down_v,
    project_v,
    text_v,
    weight_v,
    normed,
    partial,
    parts,
    pooled,
    start,
    gain_own,
    gains,
    features,
    result,
    load_sem,
    weight_sem,
    phase_send,
    phase_recv,
    start_send,
    layer_send,
    feature_sem,
    out_sem,
    token,
):
    section = lax.axis_index("section")
    me = lax.axis_index("tp")
    x, y = me // SIDE, lax.rem(me, SIDE)
    targets = [
        lax.rem(x + offset[0], SIDE) * SIDE + lax.rem(y + offset[1], SIDE) for offset in OFFSETS
    ]
    peers = [(i, targets[i]) for i, _ in FAR_FIRST if i]

    barrier = pltpu.get_barrier_semaphore()

    def greet(to_section, to):
        pl.semaphore_signal(barrier, inc=1, device_id=(to_section, to), device_id_type=MESH)

    for _, to in peers:
        greet(section, to)

    @pl.when(section > 0)
    def _():
        for i, _ in FAR_FIRST:
            greet(section - 1, targets[i])

    loads = [
        pltpu.make_async_copy(source, target, load_sem.at[i])
        for i, (source, target) in enumerate(
            (
                (patches_in, patches),
                (vit_gain_in, vit_gain),
                (layer_gain_in, layer_gain),
                (counts_in, counts),
                (dest_in, dest),
                (vit_up, up_v),
                (vit_down, down_v),
                (project, project_v),
                (text, text_v),
            )
        )
    ]
    for load in loads:
        load.start()
    for i in range(TP):
        pltpu.make_async_copy(
            weight.at[pl.ds(pl.multiple_of(targets[i] * WIDTH, WIDTH), WIDTH)],
            weight_v.at[i],
            weight_sem,
        ).start()

    for load in loads[:3]:
        load.wait()
    values = patches[...].astype(F32)
    centred = values - jnp.mean(values, axis=1, keepdims=True)
    spread = jnp.mean(centred * centred, axis=1, keepdims=True)
    normed[me] = (centred * lax.rsqrt(spread + EPSILON) * vit_gain[...][None]).astype(BF16)
    residual = jnp.mean(values, axis=0, keepdims=True)
    gain_own[...] = layer_gain[...].astype(F32)
    gains[0] = layer_gain[...].astype(F32)

    pl.semaphore_wait(barrier, TP - 1 + jnp.where(section < SECTIONS - 1, TP, 0))

    def send(source, target, recv_sem, to, sem, to_section=section):
        pltpu.make_async_remote_copy(
            src_ref=source,
            dst_ref=target,
            send_sem=sem,
            recv_sem=recv_sem,
            device_id=(to_section, to),
            device_id_type=MESH,
        ).start()

    def arrived(target, sem):
        pltpu.make_async_copy(target, target, sem).wait()

    for _, to in peers:
        send(normed.at[me], normed.at[me], phase_recv.at[0], to, phase_send.at[0])
    for i, to in peers:
        slot = slot_at_target(OFFSETS[i])
        send(gain_own, gains.at[slot], phase_recv.at[1], to, phase_send.at[1])

    loads[3].wait()
    loads[4].wait()
    loads[8].wait()
    square = (CAP, CAP)
    lane = lax.broadcasted_iota(jnp.int32, square, 1)
    line = lax.broadcasted_iota(jnp.int32, square, 0)
    places = dest[...].astype(F32)
    limit = jnp.sum(
        jnp.where(lane[:1] == section, counts[...][None].astype(F32), 0.0), axis=1, keepdims=True
    )
    live = lax.broadcasted_iota(jnp.int32, (CAP, 1), 0).astype(F32) < limit
    own_place = jnp.sum(jnp.where(line == section, places, 0.0), axis=0, keepdims=True)
    own_place = jnp.sum(jnp.where(line == lane, own_place, 0.0), axis=1, keepdims=True)
    position = lax.broadcasted_iota(jnp.int32, (CAP, ROWS), 1).astype(F32)
    own_text = jnp.dot(
        (position == own_place).astype(BF16), text_v[...], preferred_element_type=F32
    )

    loads[5].wait()
    loads[6].wait()
    arrived(normed.at[pl.ds(0, TP - 1)], phase_recv.at[0])
    whole = normed[...].reshape(TP * POOL, DV)
    hidden = jax.nn.gelu(
        jnp.dot(whole, up_v[...], preferred_element_type=F32), approximate=True
    ).astype(BF16)
    merge = lax.broadcasted_iota(jnp.int32, (TP, TP * POOL), 1) // POOL == lax.broadcasted_iota(
        jnp.int32, (TP, TP * POOL), 0
    )
    merged = jnp.dot(
        jnp.where(merge, 1.0 / POOL, 0.0).astype(BF16), hidden, preferred_element_type=F32
    )
    terms = jnp.dot(merged.astype(BF16), down_v[...], preferred_element_type=F32)
    mine = lax.broadcasted_iota(jnp.int32, (TP, DV), 0) == me
    terms = (terms + jnp.where(mine, residual, 0.0)).astype(BF16)
    for j in range(COLS):
        partial[j] = terms[:, j * LANES : (j + 1) * LANES]

    for i, to in peers:

        @pl.when(to < COLS)
        def _():
            send(partial.at[to], parts.at[me], phase_recv.at[2], to, phase_send.at[2])

    @pl.when(me < COLS)
    def _():
        parts[me] = partial[me]
        arrived(parts.at[pl.ds(0, TP - 1)], phase_recv.at[2])
        total = jnp.sum(parts[...].astype(F32), axis=0)
        block = pl.ds(pl.multiple_of(me * LANES, LANES), LANES)
        pooled[:, block] = total.astype(BF16)
        for _, to in peers:
            send(pooled.at[:, block], pooled.at[:, block], phase_recv.at[3], to, phase_send.at[3])
        arrived(pooled.at[:, pl.ds(0, (COLS - 1) * LANES)], phase_recv.at[3])

    @pl.when(me >= COLS)
    def _():
        arrived(pooled, phase_recv.at[3])

    loads[7].wait()
    embed = jnp.dot(pooled[...], project_v[...], preferred_element_type=F32).astype(BF16)

    start[...] = (
        (own_text + jnp.where(live, embed.astype(F32), 0.0)).astype(BF16).reshape(2, R, WIDTH)
    )

    def class_of(slot):
        (c,) = [c for c, (lo, hi) in enumerate(CLASSES) if lo <= slot < hi]
        return c

    def send_start(count):
        for k in range(2):
            for i, offset in FAR_FIRST[:count]:
                slot = slot_at_target(offset)
                send(
                    start.at[k],
                    features.at[2 * section + k, slot],
                    feature_sem.at[2 * section + k, class_of(slot)],
                    targets[i],
                    start_send.at[k],
                    0,
                )

    def pass_token():
        pl.semaphore_signal(token, inc=1, device_id=(section + 1, me), device_id_type=MESH)

    @pl.when(section == 0)
    def _():
        features[pl.ds(0, 2), 0] = start[...]
        send_start(TP - 1)
        pass_token()

    @pl.when(section > 0)
    def _():
        pl.semaphore_wait(token, 1)
        send_start(TP)
        arrived(features.at[0], start_send.at[0])

        @pl.when(section < SECTIONS - 1)
        def _():
            pass_token()

    arrived(gains.at[pl.ds(0, TP - 1)], phase_recv.at[1])
    arrived(weight_v, weight_sem)

    def layer(m, wait):
        product = jnp.zeros((R, WIDTH), F32)
        squares = jnp.zeros((R, LANES), F32)
        for c, (lo, hi) in enumerate(CLASSES):
            wait(c, pl.ds(lo, hi - lo))
            for i in range(lo, hi):
                part = features[m, i].astype(F32)
                for at in range(0, WIDTH, LANES):
                    squares += part[:, at : at + LANES] * part[:, at : at + LANES]
                scaled = (part * gains[i]).astype(BF16)
                product += jnp.dot(scaled, weight_v[i], preferred_element_type=F32)
        scale = lax.rsqrt(jnp.sum(squares, axis=1, keepdims=True) / D + EPSILON)
        result[m] = (features[m, 0].astype(F32) + product * scale).astype(BF16)

    def hand_on(m):
        for i, offset in FAR_FIRST:
            slot = slot_at_target(offset)
            send(
                result.at[m],
                features.at[m, slot],
                feature_sem.at[m, class_of(slot)],
                targets[i],
                layer_send.at[m * BATCHES // STEPS],
                section + 1,
            )

    def store(p):
        two = pl.ds(2 * p, 2)
        pltpu.make_async_copy(result.at[two], out.at[two], out_sem.at[0]).start()

    def pair(p, carry):
        for m in (2 * p, 2 * p + 1):

            def wait(c, slots):
                def one():
                    arrived(features.at[m, slots], feature_sem.at[m, c])

                if c:
                    one()
                else:
                    pl.when((section > 0) | (p > 0))(one)

            layer(m, wait)

            @pl.when(section < SECTIONS - 1)
            def _():
                hand_on(m)

        store(p)
        return carry

    lax.fori_loop(0, PAIRS, pair, 0)

    arrived(normed.at[pl.ds(0, TP - 1)], phase_send.at[0])
    arrived(gains.at[pl.ds(0, TP - 1)], phase_send.at[1])

    @pl.when(me < COLS)
    def _():
        arrived(partial.at[pl.ds(0, COLS - 1)], phase_send.at[2])
        arrived(parts.at[pl.ds(0, TP - 1)], phase_send.at[3])

    @pl.when(me >= COLS)
    def _():
        arrived(partial, phase_send.at[2])

    many = STEPS // BATCHES

    @pl.when(section == 0)
    def _():
        for k in range(2):
            arrived(features.at[k, pl.ds(0, TP - 1)], start_send.at[k])

    @pl.when(section > 0)
    def _():
        arrived(features.at[1], start_send.at[1])

    @pl.when(section < SECTIONS - 1)
    def _():
        for b in range(BATCHES):
            arrived(features.at[pl.ds(b * many, many)], layer_send.at[b])

    arrived(result, out_sem.at[0])


def shards(
    patches,
    vit_gain,
    vit_up,
    vit_down,
    project,
    text,
    image_counts,
    image_dest,
    layer_gain,
    layer_weight,
):
    hbm = pl.BlockSpec(memory_space=pltpu.HBM)
    dma = pltpu.SemaphoreType.DMA
    hidden = vit_up.shape[1]
    outputs = pl.pallas_call(
        kernel,
        out_shape=jax.ShapeDtypeStruct((STEPS, R, WIDTH), BF16),
        in_specs=[hbm] * 10,
        out_specs=hbm,
        scratch_shapes=[
            pltpu.VMEM(patches.shape, BF16),
            pltpu.VMEM(vit_gain.shape, F32),
            pltpu.VMEM(image_counts.shape, jnp.int32),
            pltpu.VMEM(image_dest.shape, jnp.int32),
            pltpu.VMEM(layer_gain.shape, BF16),
            pltpu.VMEM((DV, hidden), BF16),
            pltpu.VMEM((hidden, DV), BF16),
            pltpu.VMEM((DV, WIDTH), BF16),
            pltpu.VMEM((ROWS, WIDTH), BF16),
            pltpu.VMEM((TP, WIDTH, WIDTH), BF16),
            pltpu.VMEM((TP, POOL, DV), BF16),
            pltpu.VMEM((COLS, TP, LANES), BF16),
            pltpu.VMEM((TP, TP, LANES), BF16),
            pltpu.VMEM((TP, DV), BF16),
            pltpu.VMEM((2, R, WIDTH), BF16),
            pltpu.VMEM((1, WIDTH), F32),
            pltpu.VMEM((TP, 1, WIDTH), F32),
            pltpu.VMEM((STEPS, TP, R, WIDTH), BF16),
            pltpu.VMEM((STEPS, R, WIDTH), BF16),
            dma((9,)),
            dma,
            dma((4,)),
            dma((4,)),
            dma((2,)),
            dma((BATCHES,)),
            dma((STEPS, len(CLASSES))),
            dma((BATCHES,)),
            pltpu.SemaphoreType.REGULAR,
        ],
        compiler_params=pltpu.CompilerParams(
            collective_id=0, has_side_effects=True, vmem_limit_bytes=60 << 20
        ),
        cost_estimate=pl.CostEstimate(
            flops=2 * ROWS * D * WIDTH, bytes_accessed=12 << 20, transcendentals=0
        ),
        name="encoder_and_layers",
    )(
        patches,
        vit_gain,
        image_counts,
        image_dest,
        layer_gain,
        vit_up,
        vit_down,
        project,
        text,
        layer_weight[0],
    )
    slots = outputs.reshape(SECTIONS, CAP, WIDTH)
    onehot = (image_dest[:, :, None] == jnp.arange(ROWS, dtype=jnp.int32)).astype(BF16)
    ordered = lax.dot_general(
        onehot, slots, (((0, 1), (0, 1)), ((), ())), preferred_element_type=F32
    )
    return ordered.astype(BF16).reshape(1, 8, ROWS // 8, WIDTH)


def solution(mesh):
    in_specs = (
        P(("section", "tp"), None),
        P(),
        P(None, "tp"),
        P("tp", None),
        P(None, "tp"),
        P(None, "tp"),
        P(),
        P(),
        P("section", "tp"),
        P("section", None, "tp"),
    )
    out_specs = P("section", None, None, "tp")
    return jax.shard_map(shards, mesh=mesh, in_specs=in_specs, out_specs=out_specs, check_vma=False)
```

```python
import functools

import jax
import jax.numpy as jnp
from jax import lax
from jax.experimental import pallas as pl
from jax.experimental.pallas import tpu as pltpu
from jax.sharding import PartitionSpec as P

MESH = pl.DeviceIdType.MESH
F32 = jnp.float32
BF16 = jnp.bfloat16

D = 8192
DV = 1664
POOL = 4
EPSILON = 1e-05
SIDE = 4
TP = SIDE * SIDE
SECTIONS = 16
ROWS = 256
CAP = 16
WIDTH = D // TP
LANES = 128
COLS = DV // LANES
R = 8
STEPS = ROWS // R
PAIRS = STEPS // 2
EARLY = 12
BATCHES = 4


def hops(offset):
    return sum(min(o, SIDE - o) for o in offset)


OFFSETS = sorted(((a, b) for a in range(SIDE) for b in range(SIDE)), key=hops)
FAR_FIRST = list(reversed(list(enumerate(OFFSETS))))
CLASSES = [
    (lo, lo + sum(hops(o) == h for o in OFFSETS))
    for h, lo in [(hops(o), i) for i, o in enumerate(OFFSETS) if i == 0 or hops(o) != hops(OFFSETS[i - 1])]
]

ORDER = (0, 1, 3, 4, 2)


def slot_at_target(offset):
    return OFFSETS.index(tuple((SIDE - o) % SIDE for o in offset))


def kernel(
    patches_in,
    vit_gain_in,
    counts_in,
    dest_in,
    layer_gain_in,
    vit_up,
    vit_down,
    project,
    text,
    weight,
    out,
    patches,
    vit_gain,
    counts,
    dest,
    layer_gain,
    up_v,
    down_v,
    project_v,
    text_v,
    weight_v,
    normed,
    partial,
    parts,
    pooled,
    start,
    gain_own,
    gains,
    features,
    result,
    load_sem,
    weight_sem,
    phase_send,
    phase_recv,
    start_send,
    layer_send,
    feature_sem,
    out_sem,
    token,
):
    section = lax.axis_index("section")
    me = lax.axis_index("tp")
    x, y = me // SIDE, lax.rem(me, SIDE)
    targets = [
        lax.rem(x + offset[0], SIDE) * SIDE + lax.rem(y + offset[1], SIDE) for offset in OFFSETS
    ]
    peers = [(i, targets[i]) for i, _ in FAR_FIRST if i]

    barrier = pltpu.get_barrier_semaphore()

    def greet(to_section, to):
        pl.semaphore_signal(barrier, inc=1, device_id=(to_section, to), device_id_type=MESH)

    for _, to in peers:
        greet(section, to)

    @pl.when(section > 0)
    def _():
        for i, _ in FAR_FIRST:
            greet(section - 1, targets[i])

    loads = [
        pltpu.make_async_copy(source, target, load_sem.at[i])
        for i, (source, target) in enumerate(
            (
                (patches_in, patches),
                (vit_gain_in, vit_gain),
                (layer_gain_in, layer_gain),
                (counts_in, counts),
                (dest_in, dest),
                (vit_up, up_v),
                (vit_down, down_v),
                (project, project_v),
                (text, text_v),
            )
        )
    ]
    for load in loads:
        load.start()
    for i in range(TP):
        pltpu.make_async_copy(
            weight.at[pl.ds(pl.multiple_of(targets[i] * WIDTH, WIDTH), WIDTH)],
            weight_v.at[i],
            weight_sem,
        ).start()

    for load in loads[:3]:
        load.wait()
    values = patches[...].astype(F32)
    centred = values - jnp.mean(values, axis=1, keepdims=True)
    spread = jnp.mean(centred * centred, axis=1, keepdims=True)
    normed[me] = (centred * lax.rsqrt(spread + EPSILON) * vit_gain[...][None]).astype(BF16)
    residual = jnp.mean(values, axis=0, keepdims=True)
    gain_own[...] = layer_gain[...].astype(F32)
    gains[0] = layer_gain[...].astype(F32)

    pl.semaphore_wait(barrier, TP - 1 + jnp.where(section < SECTIONS - 1, TP, 0))

    def send(source, target, recv_sem, to, sem, to_section=section):
        pltpu.make_async_remote_copy(
            src_ref=source,
            dst_ref=target,
            send_sem=sem,
            recv_sem=recv_sem,
            device_id=(to_section, to),
            device_id_type=MESH,
        ).start()

    def arrived(target, sem):
        pltpu.make_async_copy(target, target, sem).wait()

    for _, to in peers:
        send(normed.at[me], normed.at[me], phase_recv.at[0], to, phase_send.at[0])
    for i, to in peers:
        slot = slot_at_target(OFFSETS[i])
        send(gain_own, gains.at[slot], phase_recv.at[1], to, phase_send.at[1])

    loads[3].wait()
    loads[4].wait()
    loads[8].wait()
    square = (CAP, CAP)
    lane = lax.broadcasted_iota(jnp.int32, square, 1)
    line = lax.broadcasted_iota(jnp.int32, square, 0)
    places = dest[...].astype(F32)
    limit = jnp.sum(
        jnp.where(lane[:1] == section, counts[...][None].astype(F32), 0.0), axis=1, keepdims=True
    )
    live = lax.broadcasted_iota(jnp.int32, (CAP, 1), 0).astype(F32) < limit
    own_place = jnp.sum(jnp.where(line == section, places, 0.0), axis=0, keepdims=True)
    own_place = jnp.sum(jnp.where(line == lane, own_place, 0.0), axis=1, keepdims=True)
    position = lax.broadcasted_iota(jnp.int32, (CAP, ROWS), 1).astype(F32)
    own_text = jnp.dot(
        (position == own_place).astype(BF16), text_v[...], preferred_element_type=F32
    )

    loads[5].wait()
    loads[6].wait()
    arrived(normed.at[pl.ds(0, TP - 1)], phase_recv.at[0])
    whole = normed[...].reshape(TP * POOL, DV)
    hidden = jax.nn.gelu(
        jnp.dot(whole, up_v[...], preferred_element_type=F32), approximate=True
    ).astype(BF16)
    merge = lax.broadcasted_iota(jnp.int32, (TP, TP * POOL), 1) // POOL == lax.broadcasted_iota(
        jnp.int32, (TP, TP * POOL), 0
    )
    merged = jnp.dot(
        jnp.where(merge, 1.0 / POOL, 0.0).astype(BF16), hidden, preferred_element_type=F32
    )
    terms = jnp.dot(merged.astype(BF16), down_v[...], preferred_element_type=F32)
    mine = lax.broadcasted_iota(jnp.int32, (TP, DV), 0) == me
    terms = (terms + jnp.where(mine, residual, 0.0)).astype(BF16)
    for j in range(COLS):
        partial[j] = terms[:, j * LANES : (j + 1) * LANES]

    for i, to in peers:

        @pl.when(to < COLS)
        def _():
            send(partial.at[to], parts.at[me], phase_recv.at[2], to, phase_send.at[2])

    @pl.when(me < COLS)
    def _():
        parts[me] = partial[me]
        arrived(parts.at[pl.ds(0, TP - 1)], phase_recv.at[2])
        total = jnp.sum(parts[...].astype(F32), axis=0)
        block = pl.ds(pl.multiple_of(me * LANES, LANES), LANES)
        pooled[:, block] = total.astype(BF16)
        for _, to in peers:
            send(pooled.at[:, block], pooled.at[:, block], phase_recv.at[3], to, phase_send.at[3])
        arrived(pooled.at[:, pl.ds(0, (COLS - 1) * LANES)], phase_recv.at[3])

    @pl.when(me >= COLS)
    def _():
        arrived(pooled, phase_recv.at[3])

    loads[7].wait()
    embed = jnp.dot(pooled[...], project_v[...], preferred_element_type=F32).astype(BF16)

    start[...] = (
        (own_text + jnp.where(live, embed.astype(F32), 0.0)).astype(BF16).reshape(2, R, WIDTH)
    )

    def class_of(slot):
        (c,) = [c for c, (lo, hi) in enumerate(CLASSES) if lo <= slot < hi]
        return c

    def send_start(count):
        for k in range(2):
            for n, (i, offset) in enumerate(FAR_FIRST[:count]):
                slot = slot_at_target(offset)
                send(
                    start.at[k],
                    features.at[2 * section + k, slot],
                    feature_sem.at[2 * section + k, class_of(slot)],
                    targets[i],
                    start_send.at[0 if k == 0 and n < EARLY else 1],
                    0,
                )

    def pass_token():
        pl.semaphore_signal(token, inc=1, device_id=(section + 1, me), device_id_type=MESH)

    @pl.when(section == 0)
    def _():
        features[pl.ds(0, 2), 0] = start[...]
        send_start(TP - 1)
        pass_token()

    @pl.when(section > 0)
    def _():
        pl.semaphore_wait(token, 1)
        send_start(TP)
        arrived(features.at[0, pl.ds(0, EARLY)], start_send.at[0])

        @pl.when(section < SECTIONS - 1)
        def _():
            pass_token()

    arrived(gains.at[pl.ds(0, TP - 1)], phase_recv.at[1])
    arrived(weight_v, weight_sem)

    def layer(m, wait):
        product = jnp.zeros((R, WIDTH), F32)
        squares = jnp.zeros((R, LANES), F32)
        for c in ORDER:
            lo, hi = CLASSES[c]
            wait(c, pl.ds(lo, hi - lo))
            for i in range(lo, hi):
                part = features[m, i].astype(F32)
                for at in range(0, WIDTH, LANES):
                    squares += part[:, at : at + LANES] * part[:, at : at + LANES]
                scaled = (part * gains[i]).astype(BF16)
                product += jnp.dot(scaled, weight_v[i], preferred_element_type=F32)
        scale = lax.rsqrt(jnp.sum(squares, axis=1, keepdims=True) / D + EPSILON)
        result[m] = (features[m, 0].astype(F32) + product * scale).astype(BF16)

    def hand_on(m):
        for i, offset in FAR_FIRST:
            slot = slot_at_target(offset)
            send(
                result.at[m],
                features.at[m, slot],
                feature_sem.at[m, class_of(slot)],
                targets[i],
                layer_send.at[m * BATCHES // STEPS],
                section + 1,
            )

    def store(p):
        two = pl.ds(2 * p, 2)
        pltpu.make_async_copy(result.at[two], out.at[two], out_sem.at[0]).start()

    def pair(p, carry):
        for m in (2 * p, 2 * p + 1):

            def wait(c, slots):
                def one():
                    arrived(features.at[m, slots], feature_sem.at[m, c])

                if c:
                    one()
                else:
                    pl.when((section > 0) | (p > 0))(one)

            layer(m, wait)

            @pl.when(section < SECTIONS - 1)
            def _():
                hand_on(m)

        store(p)
        return carry

    lax.fori_loop(0, PAIRS, pair, 0)

    arrived(normed.at[pl.ds(0, TP - 1)], phase_send.at[0])
    arrived(gains.at[pl.ds(0, TP - 1)], phase_send.at[1])

    @pl.when(me < COLS)
    def _():
        arrived(partial.at[pl.ds(0, COLS - 1)], phase_send.at[2])
        arrived(parts.at[pl.ds(0, TP - 1)], phase_send.at[3])

    @pl.when(me >= COLS)
    def _():
        arrived(partial, phase_send.at[2])

    many = STEPS // BATCHES

    @pl.when(section == 0)
    def _():
        arrived(features.at[0, pl.ds(0, EARLY)], start_send.at[0])
        arrived(features.at[0, pl.ds(EARLY, TP - 1 - EARLY)], start_send.at[1])
        arrived(features.at[1, pl.ds(0, TP - 1)], start_send.at[1])

    @pl.when(section > 0)
    def _():
        arrived(features.at[0, pl.ds(EARLY, TP - EARLY)], start_send.at[1])
        arrived(features.at[1], start_send.at[1])

    @pl.when(section < SECTIONS - 1)
    def _():
        for b in range(BATCHES):
            arrived(features.at[pl.ds(b * many, many)], layer_send.at[b])

    arrived(result, out_sem.at[0])


def shards(
    patches,
    vit_gain,
    vit_up,
    vit_down,
    project,
    text,
    image_counts,
    image_dest,
    layer_gain,
    layer_weight,
):
    hbm = pl.BlockSpec(memory_space=pltpu.HBM)
    dma = pltpu.SemaphoreType.DMA
    hidden = vit_up.shape[1]
    outputs = pl.pallas_call(
        kernel,
        out_shape=jax.ShapeDtypeStruct((STEPS, R, WIDTH), BF16),
        in_specs=[hbm] * 10,
        out_specs=hbm,
        scratch_shapes=[
            pltpu.VMEM(patches.shape, BF16),
            pltpu.VMEM(vit_gain.shape, F32),
            pltpu.VMEM(image_counts.shape, jnp.int32),
            pltpu.VMEM(image_dest.shape, jnp.int32),
            pltpu.VMEM(layer_gain.shape, BF16),
            pltpu.VMEM((DV, hidden), BF16),
            pltpu.VMEM((hidden, DV), BF16),
            pltpu.VMEM((DV, WIDTH), BF16),
            pltpu.VMEM((ROWS, WIDTH), BF16),
            pltpu.VMEM((TP, WIDTH, WIDTH), BF16),
            pltpu.VMEM((TP, POOL, DV), BF16),
            pltpu.VMEM((COLS, TP, LANES), BF16),
            pltpu.VMEM((TP, TP, LANES), BF16),
            pltpu.VMEM((TP, DV), BF16),
            pltpu.VMEM((2, R, WIDTH), BF16),
            pltpu.VMEM((1, WIDTH), F32),
            pltpu.VMEM((TP, 1, WIDTH), F32),
            pltpu.VMEM((STEPS, TP, R, WIDTH), BF16),
            pltpu.VMEM((STEPS, R, WIDTH), BF16),
            dma((9,)),
            dma,
            dma((4,)),
            dma((4,)),
            dma((2,)),
            dma((BATCHES,)),
            dma((STEPS, len(CLASSES))),
            dma((BATCHES,)),
            pltpu.SemaphoreType.REGULAR,
        ],
        compiler_params=pltpu.CompilerParams(
            collective_id=0, has_side_effects=True, vmem_limit_bytes=60 << 20
        ),
        cost_estimate=pl.CostEstimate(
            flops=2 * ROWS * D * WIDTH, bytes_accessed=12 << 20, transcendentals=0
        ),
        name="encoder_and_layers",
    )(
        patches,
        vit_gain,
        image_counts,
        image_dest,
        layer_gain,
        vit_up,
        vit_down,
        project,
        text,
        layer_weight[0],
    )
    slots = outputs.reshape(SECTIONS, CAP, WIDTH)
    onehot = (image_dest[:, :, None] == jnp.arange(ROWS, dtype=jnp.int32)).astype(BF16)
    ordered = lax.dot_general(
        onehot, slots, (((0, 1), (0, 1)), ((), ())), preferred_element_type=F32
    )
    return ordered.astype(BF16).reshape(1, 8, ROWS // 8, WIDTH)


def solution(mesh):
    in_specs = (
        P(("section", "tp"), None),
        P(),
        P(None, "tp"),
        P("tp", None),
        P(None, "tp"),
        P(None, "tp"),
        P(),
        P(),
        P("section", "tp"),
        P("section", None, "tp"),
    )
    out_specs = P("section", None, None, "tp")
    return jax.shard_map(shards, mesh=mesh, in_specs=in_specs, out_specs=out_specs, check_vma=False)
```

```python
import functools

import jax
import jax.numpy as jnp
from jax import lax
from jax.experimental import pallas as pl
from jax.experimental.pallas import tpu as pltpu
from jax.sharding import PartitionSpec as P

MESH = pl.DeviceIdType.MESH
F32 = jnp.float32
BF16 = jnp.bfloat16

D = 8192
DV = 1664
POOL = 4
EPSILON = 1e-05
SIDE = 4
TP = SIDE * SIDE
SECTIONS = 16
ROWS = 256
CAP = 16
WIDTH = D // TP
LANES = 128
COLS = DV // LANES
R = 8
STEPS = ROWS // R
PAIRS = STEPS // 2
EARLY = 12
BATCHES = 4


def hops(offset):
    return sum(min(o, SIDE - o) for o in offset)


OFFSETS = sorted(((a, b) for a in range(SIDE) for b in range(SIDE)), key=hops)
FAR_FIRST = list(reversed(list(enumerate(OFFSETS))))
CLASSES = [
    (lo, lo + sum(hops(o) == h for o in OFFSETS))
    for h, lo in [(hops(o), i) for i, o in enumerate(OFFSETS) if i == 0 or hops(o) != hops(OFFSETS[i - 1])]
]

ORDER = (0, 1, 3, 4, 2)


def slot_at_target(offset):
    return OFFSETS.index(tuple((SIDE - o) % SIDE for o in offset))


def kernel(
    patches_in,
    vit_gain_in,
    counts_in,
    dest_in,
    layer_gain_in,
    vit_up,
    vit_down,
    project,
    text,
    weight,
    out,
    patches,
    vit_gain,
    counts,
    dest,
    layer_gain,
    up_v,
    down_v,
    project_v,
    text_v,
    weight_v,
    normed,
    partial,
    parts,
    pooled,
    start,
    gain_own,
    gains,
    features,
    result,
    load_sem,
    weight_sem,
    phase_send,
    phase_recv,
    start_send,
    layer_send,
    feature_sem,
    out_sem,
    token,
):
    section = lax.axis_index("section")
    me = lax.axis_index("tp")
    x, y = me // SIDE, lax.rem(me, SIDE)
    targets = [
        lax.rem(x + offset[0], SIDE) * SIDE + lax.rem(y + offset[1], SIDE) for offset in OFFSETS
    ]
    peers = [(i, targets[i]) for i, _ in FAR_FIRST if i]

    barrier = pltpu.get_barrier_semaphore()

    def greet(to_section, to):
        pl.semaphore_signal(barrier, inc=1, device_id=(to_section, to), device_id_type=MESH)

    @pl.when(section > 0)
    def _():
        for i, _ in FAR_FIRST:
            greet(section - 1, targets[i])

    for _, to in peers:
        greet(section, to)

    loads = [
        pltpu.make_async_copy(source, target, load_sem.at[i])
        for i, (source, target) in enumerate(
            (
                (patches_in, patches),
                (vit_gain_in, vit_gain),
                (layer_gain_in, layer_gain),
                (counts_in, counts),
                (dest_in, dest),
                (vit_up, up_v),
                (vit_down, down_v),
                (project, project_v),
                (text, text_v),
            )
        )
    ]
    for load in loads:
        load.start()
    for i in range(TP):
        pltpu.make_async_copy(
            weight.at[pl.ds(pl.multiple_of(targets[i] * WIDTH, WIDTH), WIDTH)],
            weight_v.at[i],
            weight_sem,
        ).start()

    for load in loads[:3]:
        load.wait()
    values = patches[...].astype(F32)
    centred = values - jnp.mean(values, axis=1, keepdims=True)
    spread = jnp.mean(centred * centred, axis=1, keepdims=True)
    normed[me] = (centred * lax.rsqrt(spread + EPSILON) * vit_gain[...][None]).astype(BF16)
    residual = jnp.mean(values, axis=0, keepdims=True)
    gain_own[...] = layer_gain[...].astype(F32)
    gains[0] = layer_gain[...].astype(F32)

    pl.semaphore_wait(barrier, TP - 1 + jnp.where(section < SECTIONS - 1, TP, 0))

    def send(source, target, recv_sem, to, sem, to_section=section):
        pltpu.make_async_remote_copy(
            src_ref=source,
            dst_ref=target,
            send_sem=sem,
            recv_sem=recv_sem,
            device_id=(to_section, to),
            device_id_type=MESH,
        ).start()

    def arrived(target, sem):
        pltpu.make_async_copy(target, target, sem).wait()

    for _, to in peers:
        send(normed.at[me], normed.at[me], phase_recv.at[0], to, phase_send.at[0])
    for i, to in peers:
        slot = slot_at_target(OFFSETS[i])
        send(gain_own, gains.at[slot], phase_recv.at[1], to, phase_send.at[1])

    loads[3].wait()
    loads[4].wait()
    loads[8].wait()
    square = (CAP, CAP)
    lane = lax.broadcasted_iota(jnp.int32, square, 1)
    line = lax.broadcasted_iota(jnp.int32, square, 0)
    places = dest[...].astype(F32)
    limit = jnp.sum(
        jnp.where(lane[:1] == section, counts[...][None].astype(F32), 0.0), axis=1, keepdims=True
    )
    live = lax.broadcasted_iota(jnp.int32, (CAP, 1), 0).astype(F32) < limit
    own_place = jnp.sum(jnp.where(line == section, places, 0.0), axis=0, keepdims=True)
    own_place = jnp.sum(jnp.where(line == lane, own_place, 0.0), axis=1, keepdims=True)
    position = lax.broadcasted_iota(jnp.int32, (CAP, ROWS), 1).astype(F32)
    own_text = jnp.dot(
        (position == own_place).astype(BF16), text_v[...], preferred_element_type=F32
    )

    loads[5].wait()
    loads[6].wait()
    arrived(normed.at[pl.ds(0, TP - 1)], phase_recv.at[0])
    whole = normed[...].reshape(TP * POOL, DV)
    hidden = jax.nn.gelu(
        jnp.dot(whole, up_v[...], preferred_element_type=F32), approximate=True
    ).astype(BF16)
    merge = lax.broadcasted_iota(jnp.int32, (TP, TP * POOL), 1) // POOL == lax.broadcasted_iota(
        jnp.int32, (TP, TP * POOL), 0
    )
    merged = jnp.dot(
        jnp.where(merge, 1.0 / POOL, 0.0).astype(BF16), hidden, preferred_element_type=F32
    )
    terms = jnp.dot(merged.astype(BF16), down_v[...], preferred_element_type=F32)
    mine = lax.broadcasted_iota(jnp.int32, (TP, DV), 0) == me
    terms = (terms + jnp.where(mine, residual, 0.0)).astype(BF16)
    for j in range(COLS):
        partial[j] = terms[:, j * LANES : (j + 1) * LANES]

    for i, to in peers:

        @pl.when(to < COLS)
        def _():
            send(partial.at[to], parts.at[me], phase_recv.at[2], to, phase_send.at[2])

    @pl.when(me < COLS)
    def _():
        parts[me] = partial[me]
        arrived(parts.at[pl.ds(0, TP - 1)], phase_recv.at[2])
        total = jnp.sum(parts[...].astype(F32), axis=0)
        block = pl.ds(pl.multiple_of(me * LANES, LANES), LANES)
        pooled[:, block] = total.astype(BF16)
        for _, to in peers:
            send(pooled.at[:, block], pooled.at[:, block], phase_recv.at[3], to, phase_send.at[3])
        arrived(pooled.at[:, pl.ds(0, (COLS - 1) * LANES)], phase_recv.at[3])

    @pl.when(me >= COLS)
    def _():
        arrived(pooled, phase_recv.at[3])

    loads[7].wait()
    embed = jnp.dot(pooled[...], project_v[...], preferred_element_type=F32).astype(BF16)

    start[...] = (
        (own_text + jnp.where(live, embed.astype(F32), 0.0)).astype(BF16).reshape(2, R, WIDTH)
    )

    def class_of(slot):
        (c,) = [c for c, (lo, hi) in enumerate(CLASSES) if lo <= slot < hi]
        return c

    def send_start(count):
        for k in range(2):
            for n, (i, offset) in enumerate(FAR_FIRST[:count]):
                slot = slot_at_target(offset)
                send(
                    start.at[k],
                    features.at[2 * section + k, slot],
                    feature_sem.at[2 * section + k, class_of(slot)],
                    targets[i],
                    start_send.at[0 if k == 0 and n < EARLY else 1],
                    0,
                )

    def pass_token():
        pl.semaphore_signal(token, inc=1, device_id=(section + 1, me), device_id_type=MESH)

    @pl.when(section == 0)
    def _():
        features[pl.ds(0, 2), 0] = start[...]
        send_start(TP - 1)
        pass_token()

    @pl.when(section > 0)
    def _():
        pl.semaphore_wait(token, 1)
        send_start(TP)
        arrived(features.at[0, pl.ds(0, EARLY)], start_send.at[0])

        @pl.when(section < SECTIONS - 1)
        def _():
            pass_token()

    arrived(gains.at[pl.ds(0, TP - 1)], phase_recv.at[1])
    arrived(weight_v, weight_sem)

    def layer(m, wait):
        product = jnp.zeros((R, WIDTH), F32)
        squares = jnp.zeros((R, LANES), F32)
        for c in ORDER:
            lo, hi = CLASSES[c]
            wait(c, pl.ds(lo, hi - lo))
            for i in range(lo, hi):
                part = features[m, i].astype(F32)
                for at in range(0, WIDTH, LANES):
                    squares += part[:, at : at + LANES] * part[:, at : at + LANES]
                scaled = (part * gains[i]).astype(BF16)
                product += jnp.dot(scaled, weight_v[i], preferred_element_type=F32)
        scale = lax.rsqrt(jnp.sum(squares, axis=1, keepdims=True) / D + EPSILON)
        result[m] = (features[m, 0].astype(F32) + product * scale).astype(BF16)

    def hand_on(m):
        for i, offset in FAR_FIRST:
            slot = slot_at_target(offset)
            send(
                result.at[m],
                features.at[m, slot],
                feature_sem.at[m, class_of(slot)],
                targets[i],
                layer_send.at[m * BATCHES // STEPS],
                section + 1,
            )

    def store(p):
        two = pl.ds(2 * p, 2)
        pltpu.make_async_copy(result.at[two], out.at[two], out_sem.at[0]).start()

    def pair(p, carry):
        for m in (2 * p, 2 * p + 1):

            def wait(c, slots):
                def one():
                    arrived(features.at[m, slots], feature_sem.at[m, c])

                if c:
                    one()
                else:
                    pl.when((section > 0) | (p > 0))(one)

            layer(m, wait)

            @pl.when(section < SECTIONS - 1)
            def _():
                hand_on(m)

        store(p)
        return carry

    lax.fori_loop(0, PAIRS, pair, 0)

    arrived(normed.at[pl.ds(0, TP - 1)], phase_send.at[0])
    arrived(gains.at[pl.ds(0, TP - 1)], phase_send.at[1])

    @pl.when(me < COLS)
    def _():
        arrived(partial.at[pl.ds(0, COLS - 1)], phase_send.at[2])
        arrived(parts.at[pl.ds(0, TP - 1)], phase_send.at[3])

    @pl.when(me >= COLS)
    def _():
        arrived(partial, phase_send.at[2])

    many = STEPS // BATCHES

    @pl.when(section == 0)
    def _():
        arrived(features.at[0, pl.ds(0, EARLY)], start_send.at[0])
        arrived(features.at[0, pl.ds(EARLY, TP - 1 - EARLY)], start_send.at[1])
        arrived(features.at[1, pl.ds(0, TP - 1)], start_send.at[1])

    @pl.when(section > 0)
    def _():
        arrived(features.at[0, pl.ds(EARLY, TP - EARLY)], start_send.at[1])
        arrived(features.at[1], start_send.at[1])

    @pl.when(section < SECTIONS - 1)
    def _():
        for b in range(BATCHES):
            arrived(features.at[pl.ds(b * many, many)], layer_send.at[b])

    arrived(result, out_sem.at[0])


def shards(
    patches,
    vit_gain,
    vit_up,
    vit_down,
    project,
    text,
    image_counts,
    image_dest,
    layer_gain,
    layer_weight,
):
    hbm = pl.BlockSpec(memory_space=pltpu.HBM)
    dma = pltpu.SemaphoreType.DMA
    hidden = vit_up.shape[1]
    outputs = pl.pallas_call(
        kernel,
        out_shape=jax.ShapeDtypeStruct((STEPS, R, WIDTH), BF16),
        in_specs=[hbm] * 10,
        out_specs=hbm,
        scratch_shapes=[
            pltpu.VMEM(patches.shape, BF16),
            pltpu.VMEM(vit_gain.shape, F32),
            pltpu.VMEM(image_counts.shape, jnp.int32),
            pltpu.VMEM(image_dest.shape, jnp.int32),
            pltpu.VMEM(layer_gain.shape, BF16),
            pltpu.VMEM((DV, hidden), BF16),
            pltpu.VMEM((hidden, DV), BF16),
            pltpu.VMEM((DV, WIDTH), BF16),
            pltpu.VMEM((ROWS, WIDTH), BF16),
            pltpu.VMEM((TP, WIDTH, WIDTH), BF16),
            pltpu.VMEM((TP, POOL, DV), BF16),
            pltpu.VMEM((COLS, TP, LANES), BF16),
            pltpu.VMEM((TP, TP, LANES), BF16),
            pltpu.VMEM((TP, DV), BF16),
            pltpu.VMEM((2, R, WIDTH), BF16),
            pltpu.VMEM((1, WIDTH), F32),
            pltpu.VMEM((TP, 1, WIDTH), F32),
            pltpu.VMEM((STEPS, TP, R, WIDTH), BF16),
            pltpu.VMEM((STEPS, R, WIDTH), BF16),
            dma((9,)),
            dma,
            dma((4,)),
            dma((4,)),
            dma((2,)),
            dma((BATCHES,)),
            dma((STEPS, len(CLASSES))),
            dma((BATCHES,)),
            pltpu.SemaphoreType.REGULAR,
        ],
        compiler_params=pltpu.CompilerParams(
            collective_id=0, has_side_effects=True, vmem_limit_bytes=60 << 20
        ),
        cost_estimate=pl.CostEstimate(
            flops=2 * ROWS * D * WIDTH, bytes_accessed=12 << 20, transcendentals=0
        ),
        name="encoder_and_layers",
    )(
        patches,
        vit_gain,
        image_counts,
        image_dest,
        layer_gain,
        vit_up,
        vit_down,
        project,
        text,
        layer_weight[0],
    )
    slots = outputs.reshape(SECTIONS, CAP, WIDTH)
    onehot = (image_dest[:, :, None] == jnp.arange(ROWS, dtype=jnp.int32)).astype(BF16)
    ordered = lax.dot_general(
        onehot, slots, (((0, 1), (0, 1)), ((), ())), preferred_element_type=F32
    )
    return ordered.astype(BF16).reshape(1, 8, ROWS // 8, WIDTH)


def solution(mesh):
    in_specs = (
        P(("section", "tp"), None),
        P(),
        P(None, "tp"),
        P("tp", None),
        P(None, "tp"),
        P(None, "tp"),
        P(),
        P(),
        P("section", "tp"),
        P("section", None, "tp"),
    )
    out_specs = P("section", None, None, "tp")
    return jax.shard_map(shards, mesh=mesh, in_specs=in_specs, out_specs=out_specs, check_vma=False)
```
